512 devices in a mesh: sec: 32 (over y, x, core), env: 16 (over z).
Axes of the slice: x: 4, y: 4, z: 16, core: 2. Of those that a mesh axis runs over, the one named last changes fastest.
Arguments:
- wavefunction: float32 [32, 512, 512], P('sec', 'env'), may hold values from -14 to 14
- left_env: bfloat16 [34, 512, 512], P(None, 'env'), may hold values from -0.176776695 to 0.176776695
- right_env: bfloat16 [34, 512, 512], P(None, 'env'), may hold values from -0.25 to 0.25
- task_in: int32 [512], replicated, may hold values from 0 to 31
- task_out: int32 [512, 1], replicated, may hold values from 0 to 31; in each aligned block of 512 rows (0 to 511, 512 to 1023, ...) at most 64 rows name the same one
- task_term: int32 [512], replicated, may hold values from 0 to 33
Outputs:
- sigma: float32 [32, 512, 512], P('sec', 'env')
The draws below stay inside these ranges and needn't reach their ends.
Inputs may be any that keep to these rules, and one draw needn't show every extreme that they name: `task_out`: no sector is the target of more than 64 tasks, and in every draw some sector is the target of exactly 64.
All inputs are finite; a program needn't handle non-finite values.
Results may differ from the reference program's by a relative error of at most 0.00045.
Values may be sent and summed in bfloat16 or wider, within the bound.
A program may use at most 64 MiB of HBM per device.

```python
import math
import jax
import jax.numpy as jnp
import numpy as np
from jax import lax

M = 512
TERMS = 34
CAP = 64
SECTORS = 32
TASKS = 512


def draw_wavefunction(key, part):
    offset_key, noise_key = jax.random.split(jax.random.fold_in(key, 11))
    offset = 8.0 * jax.random.uniform(offset_key, (SECTORS, 1, M), jnp.float32, -1.0, 1.0)
    noise_part = jnp.clip(jax.random.normal(noise_key, (SECTORS, M, M), jnp.float32), -4.0, 4.0)
    return (offset + noise_part).astype(jnp.float32)


def draw_left_env(key, part):
    entry_scale = 1.0 / math.sqrt(M)
    base_key = jax.random.fold_in(key, 23)
    base_draw = entry_scale * jax.random.normal(base_key, (TERMS, M, M), jnp.float32)
    centered = base_draw - 0.98 * jnp.mean(base_draw, axis=2, keepdims=True)
    return jnp.clip(centered, -4.0 * entry_scale, 4.0 * entry_scale).astype(jnp.bfloat16)


def set_ends(entries, stream_key, smallest, top_value):
    dims = entries.shape
    place = [jax.random.randint(jax.random.fold_in(stream_key, axis), (), 0, dims[axis]) for axis in range(len(dims))]
    entries = entries.at[tuple(place)].set(smallest)
    longest = dims.index(max(dims))
    place[longest] = (place[longest] + 1) % dims[longest]
    return entries.at[tuple(place)].set(top_value)


def block_scale(rng, extent, pieces, least, high):
    def one(axis_at, shards_of):
        heights = jax.random.uniform(jax.random.fold_in(jax.random.fold_in(rng, 6), axis_at), (shards_of,), jnp.float32, least / len(pieces), high / len(pieces))
        return jnp.repeat(jnp.exp(heights), extent[axis_at] // shards_of).reshape((-1,) + (1,) * (len(extent) - axis_at - 1))

    gain = one(*pieces[0])
    for cut in pieces[1:]:
        gain = gain * one(*cut)
    return gain


def assign_block(stream_key, own, number, rows, count, top, limit, slope):
    sequence = jax.random.permutation(stream_key, count)
    packed, common = shares(count, rows * top, limit, slope, True), shares(count, rows * top, limit, slope, False)
    places = jnp.arange(count)

    def named(sizes, turn):
        used = int((sizes > 0).sum())
        fixed = max(1, used // 4)
        shifted = fixed + (places - fixed + turn * (used - fixed)) % max(1, count - fixed)
        return jnp.zeros((count,), jnp.int32).at[sequence[jnp.where(places < fixed, places, shifted)]].set(jnp.asarray(sizes, jnp.int32))

    sizes = jnp.where(number % 4 == 0, named(packed, number // 4), named(common, number - number // 4 - 1))
    mixed = jax.random.permutation(jax.random.fold_in(own, 3), count)
    source_of, sink = mixed[0:count // 2 * 2:2], mixed[1:count // 2 * 2:2]
    slack = jnp.minimum(sizes[source_of] - 1, limit - sizes[sink]) // 2
    slack = jnp.where((source_of == sequence[0]) | (sink == sequence[0]) | (sizes[sink] == 0), 0, jnp.maximum(slack, 0))
    shifted = jax.random.randint(jax.random.fold_in(own, 4), (count // 2,), 0, 1 << 20) % (slack + 1)
    sizes = sizes.at[source_of].add(-shifted).at[sink].add(shifted)
    members = jnp.searchsorted(jnp.cumsum(sizes), jnp.arange(rows * top), side="right").astype(jnp.int32)
    listing = members.reshape(top, rows).T
    listing = listing[jax.random.permutation(jax.random.fold_in(own, 1), rows)]
    turn = jax.random.randint(jax.random.fold_in(own, 2), (rows, 1), 0, top)
    return jnp.take_along_axis(listing, (jnp.arange(top)[None, :] + turn) % top, axis=1)


def shares(count, total, most, skew, full):
    portions = [(1 << 20) // math.isqrt(standing ** skew) + 1 for standing in range(1, count + 1)]
    largest = most if full else min(most, max(-(-total // count), total * portions[0] // sum(portions)))
    least = 1 if total - largest >= count - 1 else 0
    given, surplus = [largest] + [least] * (count - 1), total - largest - least * (count - 1)
    while surplus > 0:
        free = [i for i in range(1, count) if given[i] < largest] or [i for i in range(1, count) if given[i] < most]
        mass, left = sum([portions[i] for i in free]), surplus
        for i in free:
            addition = min(most - given[i], max(1, left * portions[i] // mass), surplus)
            given[i] = given[i] + addition
            surplus = surplus - addition
    return np.array(given)


def normal_values(own_key, shape, scale, bound, cuts=(), dtype=jnp.bfloat16):
    values = scale * jax.random.normal(own_key, shape, jnp.float32)
    if cuts:
        values = values * block_scale(own_key, shape, cuts, -0.22, 0.18)
    return jnp.clip(values, -bound, bound).astype(dtype)


def setup_inputs(seed: int = 0) -> dict:
    arg_keys = jax.random.split(jax.random.key(seed), 7)
    wavefunction = draw_wavefunction(jax.random.fold_in(arg_keys[6], 71), 0)
    left_env = draw_left_env(jax.random.fold_in(arg_keys[6], 71), 0)
    right_env = normal_values(arg_keys[2], (TERMS, M, M), M ** -0.5, 0.25, ((1, 16),))
    task_in = set_ends(jax.random.randint(arg_keys[3], (TASKS,), 0, SECTORS), jax.random.fold_in(arg_keys[3], 1), 0, SECTORS - 1).astype(jnp.int32)
    task_out_keys = jax.random.split(jax.random.fold_in(arg_keys[4], 1), TASKS // TASKS)
    task_out_turns = jax.random.permutation(jax.random.fold_in(arg_keys[4], 3), TASKS // TASKS)
    task_out = jax.vmap(lambda own, number: assign_block(jax.random.fold_in(arg_keys[4], 2), own, number, TASKS, SECTORS, 1, CAP, 2))(task_out_keys, task_out_turns).reshape((TASKS, 1))
    task_term = set_ends(jax.random.randint(arg_keys[5], (TASKS,), 0, TERMS), jax.random.fold_in(arg_keys[5], 1), 0, TERMS - 1).astype(jnp.int32)
    return dict(wavefunction=wavefunction, left_env=left_env, right_env=right_env, task_in=task_in, task_out=task_out, task_term=task_term)


def reference(wavefunction, left_env, right_env, task_in, task_out, task_term):
    def one_task(task_id, totals):
        source = lax.dynamic_index_in_dim(wavefunction, task_in[task_id], 0, keepdims=False)
        term_id = task_term[task_id]
        left_block = lax.dynamic_index_in_dim(left_env, term_id, 0, keepdims=False).astype(jnp.float32)
        right_block = lax.dynamic_index_in_dim(right_env, term_id, 0, keepdims=False).astype(jnp.float32)
        high_part = lax.optimization_barrier(source.astype(jnp.bfloat16))
        low_part = (source - high_part.astype(jnp.float32)).astype(jnp.bfloat16)
        split_sum = high_part.astype(jnp.float32) + low_part.astype(jnp.float32)
        mixed_sum = jnp.dot(split_sum, right_block, precision=lax.Precision.HIGHEST)
        top_part = lax.optimization_barrier(mixed_sum.astype(jnp.bfloat16))
        rest_part = (mixed_sum - top_part.astype(jnp.float32)).astype(jnp.bfloat16)
        joined = top_part.astype(jnp.float32) + rest_part.astype(jnp.float32)
        result = jnp.dot(left_block, joined, precision=lax.Precision.HIGHEST)
        target = task_out[task_id, 0]
        current = lax.dynamic_index_in_dim(totals, target, 0, keepdims=True)
        return lax.dynamic_update_index_in_dim(totals, current + result[None], target, 0)

    start_totals = jnp.zeros((SECTORS, M, M), jnp.float32)
    return lax.fori_loop(0, TASKS, one_task, start_totals)
```

```python
import functools

import jax
import jax.numpy as jnp
from jax import lax
from jax.experimental import pallas as pl
from jax.experimental.pallas import tpu as pltpu
from jax.sharding import PartitionSpec as P

MESH = pl.DeviceIdType.MESH
F32 = jnp.float32
BF16 = jnp.bfloat16


def vmem():
    return pl.BlockSpec(memory_space=pltpu.VMEM)


def gather_kernel(groups, ring, psi_ref, left_ref, right_ref, q_ref, rt_ref, t_scr, send_buf, got, hl, rg, rrow,
                  a_send, a_recv, z_send, z_recv):
    g = lax.axis_index("sec")
    e = lax.axis_index("env")
    terms = left_ref.shape[0]
    rows = psi_ref.shape[1]
    cols = psi_ref.shape[2]
    per = cols // groups
    right = lax.rem(e + 1, ring)
    left = lax.rem(e + ring - 1, ring)

    barrier = pltpu.get_barrier_semaphore()
    for d in range(1, groups):
        pl.semaphore_signal(barrier, inc=1, device_id={"sec": lax.rem(g + d, groups)}, device_id_type=MESH)
    for to in (left, right):
        pl.semaphore_signal(barrier, inc=1, device_id={"env": to}, device_id_type=MESH)

    psi = psi_ref[0]
    high = psi.astype(BF16)
    low = (psi - high.astype(F32)).astype(BF16)
    stacked = jnp.concatenate(
        [high.astype(F32), low.astype(F32), jnp.zeros((128 - 2 * rows, cols), F32)], axis=0
    )
    t_scr[...] = stacked.T
    for p in range(groups):
        send_buf[p] = t_scr[pl.ds(p, per, stride=groups), :].astype(BF16)

    pl.semaphore_wait(barrier, groups + 1)

    spread = []
    for d in range(1, groups):
        to = lax.rem(g + d, groups)
        copy = pltpu.make_async_remote_copy(
            src_ref=send_buf.at[to],
            dst_ref=got.at[g],
            send_sem=a_send.at[d],
            recv_sem=a_recv.at[d],
            device_id={"sec": to},
            device_id_type=MESH,
        )
        copy.start()
        spread.append(copy)
    got[g] = send_buf[g]

    rrow[...] = jnp.zeros_like(rrow)
    pick = lax.broadcasted_iota(jnp.int32, (rows, cols), 0) == g
    for w in range(terms):
        row = jnp.sum(jnp.where(pick, right_ref[w].astype(F32), 0.0), axis=0, keepdims=True)
        rrow[pl.ds(w, 1), :] = row
    rg[e] = rrow[...].astype(BF16)

    for copy in spread:
        copy.wait_recv()
    back = got[...].astype(F32).reshape(groups * per, 128).T
    hl[e] = back[: 2 * rows].astype(BF16)

    def z_copy(buffer, slot, to, index):
        return pltpu.make_async_remote_copy(
            src_ref=buffer.at[slot],
            dst_ref=buffer.at[slot],
            send_sem=z_send.at[index],
            recv_sem=z_recv.at[index],
            device_id={"env": to},
            device_id_type=MESH,
        )

    ways = ((right, -1, ring // 2), (left, 1, ring // 2 - 1))
    flights = {}
    for h in range(ring // 2):
        for b, buffer in enumerate((hl, rg)):
            for way, (to, sign, hops) in enumerate(ways):
                if h > 0 and (way, b, h - 1) in flights:
                    flights[way, b, h - 1].wait_recv()
                if h < hops:
                    slot = lax.rem(e + sign * h + ring, ring)
                    copy = z_copy(buffer, slot, to, (b * 2 + way) * (ring // 2) + h)
                    copy.start()
                    flights[way, b, h] = copy
    for b in range(2):
        flights[0, b, ring // 2 - 1].wait_recv()

    block = cols // 2
    lanes = q_ref.shape[3]
    lhs = left_ref[...].reshape(terms * rows, cols)
    for half in range(2):
        x_high = hl[:, :rows, half * block : (half + 1) * block].reshape(ring * rows, block)
        x_low = hl[:, rows:, half * block : (half + 1) * block].reshape(ring * rows, block)
        q = jnp.dot(lhs, x_high, preferred_element_type=F32) + jnp.dot(lhs, x_low, preferred_element_type=F32)
        for part in range(block // lanes):
            q_ref[:, half * (block // lanes) + part] = q[:, part * lanes : (part + 1) * lanes].reshape(
                terms, rows, lanes
            )

    padded = rg.shape[1]
    out_row = lax.broadcasted_iota(jnp.int32, (rt_ref.shape[0], ring * padded), 0)
    in_row = lax.broadcasted_iota(jnp.int32, (rt_ref.shape[0], ring * padded), 1)
    same = (out_row // ring == in_row % padded) & (out_row % ring == in_row // padded) & (out_row < terms * ring)
    order = jnp.where(same, 1.0, 0.0).astype(BF16)
    rt_ref[...] = jnp.dot(order, rg[...].reshape(ring * padded, cols), preferred_element_type=F32).astype(BF16)

    for copy in spread:
        copy.wait_send()
    for copy in flights.values():
        copy.wait_send()


def combine_kernel(unroll, q_ref, rt_ref, in_ref, out_ref, term_ref, p_ref, b_ref):
    tasks = in_ref.shape[0]
    lanes = q_ref.shape[3]
    per = lanes // 8
    b_ref[...] = jnp.zeros_like(b_ref)
    group = lax.broadcasted_iota(jnp.int32, q_ref.shape[2:], 1) // per

    def step(n, carry):
        moved = []
        for u in range(unroll):
            t = n * unroll + u
            s, w, r = in_ref[t], term_ref[t], out_ref[t]
            block = q_ref[w, s // 8]
            shift = ((w - s + 64) % 8) * per
            block = pltpu.roll(block, shift, axis=1)
            moved.append((r, w // 8, jnp.where(group == w % 8, block, 0.0)))
        for r, tile, block in moved:
            b_ref[r, tile] = b_ref[r, tile] + block
        return carry

    lax.fori_loop(0, tasks // unroll, step, 0)

    sectors, tiles, rows, _ = b_ref.shape
    chunk = 8
    for c in range(sectors // chunk):
        b = jnp.concatenate([b_ref[c * chunk : (c + 1) * chunk, k] for k in range(tiles)], axis=2)
        b = b.reshape(chunk * rows, tiles * lanes)
        top = b.astype(BF16)
        rest = (b - top.astype(F32)).astype(BF16)
        p = jnp.dot(top, rt_ref[...], preferred_element_type=F32) + jnp.dot(
            rest, rt_ref[...], preferred_element_type=F32
        )
        p_ref[c * (chunk // 2) : (c + 1) * (chunk // 2)] = p.reshape(chunk // 2, 2, rows, p.shape[1])


def scatter_kernel(p_ref, o_ref, pair, acc, xa, yb, ca, cb, ya, xb, send, recv):
    g = lax.axis_index("sec")
    core = lax.rem(g, 2)
    x = lax.rem(g // 2, 4)
    y = g // 8
    sibling = g + 1 - 2 * core
    half = o_ref.shape[1] // 2

    def x_peer(d):
        return (y * 4 + lax.rem(x + d, 4)) * 2 + core

    def y_peer(d):
        return (lax.rem(y + d, 4) * 4 + x) * 2 + core

    barrier = pltpu.get_barrier_semaphore()
    peers = [sibling] + [x_peer(d) for d in (1, 2, 3)] + [y_peer(d) for d in (1, 2, 3)]
    for to in peers:
        pl.semaphore_signal(barrier, inc=1, device_id={"sec": to}, device_id_type=MESH)
    pl.semaphore_wait(barrier, len(peers))

    def copy(src, dst, index, to):
        made = pltpu.make_async_remote_copy(
            src_ref=src,
            dst_ref=dst,
            send_sem=send.at[index],
            recv_sem=recv.at[index],
            device_id={"sec": to},
            device_id_type=MESH,
        )
        made.start()
        return made

    tops = slice(0, half), slice(half, 2 * half)
    first = [
        copy(p_ref.at[:, 1 - core, pl.ds(k * half, half)], pair.at[k], k, sibling) for k in range(2)
    ]
    second, third = [], []
    for k in range(2):
        first[k].wait_recv()
        acc[k] = (p_ref[:, core, tops[k]] + pair[k]).reshape(acc.shape[1:])
        for d in (1, 2, 3):
            index = 2 + k * 3 + d - 1
            if k == 0:
                second.append(copy(acc.at[0, :, lax.rem(x + d, 4)], xa.at[d - 1], index, x_peer(d)))
            else:
                second.append(copy(acc.at[1, lax.rem(y + d, 4)], yb.at[d - 1], index, y_peer(d)))
    for k in range(2):
        for d in (1, 2, 3):
            second[k * 3 + d - 1].wait_recv()
        if k == 0:
            ca[...] = acc[0, :, x] + xa[0] + xa[1] + xa[2]
        else:
            cb[...] = acc[1, y] + yb[0] + yb[1] + yb[2]
        for d in (1, 2, 3):
            index = 8 + k * 3 + d - 1
            if k == 0:
                third.append(copy(ca.at[lax.rem(y + d, 4)], ya.at[d - 1], index, y_peer(d)))
            else:
                third.append(copy(cb.at[lax.rem(x + d, 4)], xb.at[d - 1], index, x_peer(d)))
    for k in range(2):
        for d in (1, 2, 3):
            third[k * 3 + d - 1].wait_recv()
        if k == 0:
            o_ref[0, :half] = ca[y] + ya[0] + ya[1] + ya[2]
        else:
            o_ref[0, half:] = cb[x] + xb[0] + xb[1] + xb[2]
    for made in first + second + third:
        made.wait_send()


def body(wavefunction, left_env, right_env, task_in, task_out, task_term):
    groups = lax.axis_size("sec")
    ring = lax.axis_size("env")
    _, rows, cols = wavefunction.shape
    terms = left_env.shape[0]
    per = cols // groups
    padded = -(-terms // 16) * 16
    tiles = -(-terms // 8)
    limit = 48 * 2**20
    sems = pltpu.SemaphoreType.DMA

    q, rt = pl.pallas_call(
        functools.partial(gather_kernel, groups, ring),
        out_shape=(
            jax.ShapeDtypeStruct((terms, groups // 8, rows, 128), F32),
            jax.ShapeDtypeStruct((tiles * 128, cols), BF16),
        ),
        in_specs=[vmem()] * 3,
        out_specs=(vmem(), vmem()),
        scratch_shapes=[
            pltpu.VMEM((cols, 128), F32),
            pltpu.VMEM((groups, per, 128), BF16),
            pltpu.VMEM((groups, per, 128), BF16),
            pltpu.VMEM((ring, 2 * rows, cols), BF16),
            pltpu.VMEM((ring, padded, cols), BF16),
            pltpu.VMEM((padded, cols), F32),
            sems((groups,)),
            sems((groups,)),
            sems((2 * ring,)),
            sems((2 * ring,)),
        ],
        compiler_params=pltpu.CompilerParams(collective_id=0, has_side_effects=True, vmem_limit_bytes=limit),
        name="gather_psi",
    )(wavefunction, left_env, right_env)

    smem = pl.BlockSpec(memory_space=pltpu.SMEM)
    partial = pl.pallas_call(
        functools.partial(combine_kernel, 8),
        out_shape=jax.ShapeDtypeStruct((groups // 2, 2, rows, cols), F32),
        in_specs=[vmem(), vmem(), smem, smem, smem],
        out_specs=vmem(),
        scratch_shapes=[pltpu.VMEM((groups, tiles, rows, 128), F32)],
        compiler_params=pltpu.CompilerParams(vmem_limit_bytes=limit),
        name="combine_tasks",
    )(q, rt, task_in, task_out[:, 0], task_term)

    half = rows // 2
    return pl.pallas_call(
        scatter_kernel,
        out_shape=jax.ShapeDtypeStruct((1, rows, cols), F32),
        in_specs=[vmem()],
        out_specs=vmem(),
        scratch_shapes=[
            pltpu.VMEM((2, 16, half, cols), F32),
            pltpu.VMEM((2, 4, 4, half, cols), F32),
            pltpu.VMEM((3, 4, half, cols), F32),
            pltpu.VMEM((3, 4, half, cols), F32),
            pltpu.VMEM((4, half, cols), F32),
            pltpu.VMEM((4, half, cols), F32),
            pltpu.VMEM((3, half, cols), F32),
            pltpu.VMEM((3, half, cols), F32),
            sems((14,)),
            sems((14,)),
        ],
        compiler_params=pltpu.CompilerParams(collective_id=1, has_side_effects=True, vmem_limit_bytes=limit),
        name="scatter_sums",
    )(partial)


def solution(mesh):
    placed = (P("sec", "env", None), P(None, "env", None), P(None, "env", None), P(), P(), P())
    return jax.shard_map(
        body, mesh=mesh, in_specs=placed, out_specs=P("sec", "env", None), check_vma=False
    )
```

```python
import functools

import jax
import jax.numpy as jnp
from jax import lax
from jax.experimental import pallas as pl
from jax.experimental.pallas import tpu as pltpu
from jax.sharding import PartitionSpec as P

MESH = pl.DeviceIdType.MESH
F32 = jnp.float32
BF16 = jnp.bfloat16


def vmem():
    return pl.BlockSpec(memory_space=pltpu.VMEM)


def gather_kernel(groups, ring, psi_hbm, left_hbm, right_hbm, in_hbm, out_hbm, term_hbm, q_ref, rt_ref, pk_ref,
                  psi_ref, left_ref, right_ref, ids, t_scr, send_buf, got, hl, rg, rrow,
                  a_send, a_recv, z_send, z_recv, local):
    g = lax.axis_index("sec")
    e = lax.axis_index("env")
    terms = left_ref.shape[0]
    rows = psi_ref.shape[1]
    cols = psi_ref.shape[2]
    per = cols // groups
    right = lax.rem(e + 1, ring)
    left = lax.rem(e + ring - 1, ring)

    loads = [
        pltpu.make_async_copy(src, dst, local.at[n])
        for n, (src, dst) in enumerate(
            (
                (psi_hbm, psi_ref),
                (right_hbm, right_ref),
                (in_hbm, ids.at[0]),
                (out_hbm, ids.at[1]),
                (term_hbm, ids.at[2]),
                (left_hbm, left_ref),
            )
        )
    ]
    for load in loads:
        load.start()

    barrier = pltpu.get_barrier_semaphore()
    for d in range(1, groups):
        pl.semaphore_signal(barrier, inc=1, device_id={"sec": lax.rem(g + d, groups)}, device_id_type=MESH)
    for to in (left, right):
        pl.semaphore_signal(barrier, inc=1, device_id={"env": to}, device_id_type=MESH)

    loads[0].wait()
    psi = psi_ref[0]
    high = psi.astype(BF16)
    low = (psi - high.astype(F32)).astype(BF16)
    stacked = jnp.concatenate(
        [high.astype(F32), low.astype(F32), jnp.zeros((128 - 2 * rows, cols), F32)], axis=0
    )
    t_scr[...] = stacked.T
    for p in range(groups):
        send_buf[p] = t_scr[pl.ds(p, per, stride=groups), :].astype(BF16)

    pl.semaphore_wait(barrier, groups + 1)

    spread = []
    for d in range(1, groups):
        to = lax.rem(g + d, groups)
        copy = pltpu.make_async_remote_copy(
            src_ref=send_buf.at[to],
            dst_ref=got.at[g],
            send_sem=a_send.at[d],
            recv_sem=a_recv.at[d],
            device_id={"sec": to},
            device_id_type=MESH,
        )
        copy.start()
        spread.append(copy)
    got[g] = send_buf[g]

    loads[1].wait()
    rrow[...] = jnp.zeros_like(rrow)
    pick = lax.broadcasted_iota(jnp.int32, (rows, cols), 0) == g
    for w in range(terms):
        row = jnp.sum(jnp.where(pick, right_ref[w].astype(F32), 0.0), axis=0, keepdims=True)
        rrow[pl.ds(w, 1), :] = row
    rg[e] = rrow[...].astype(BF16)

    steps = ring // 2
    ways = ((right, -1, steps), (left, 1, steps - 1))
    flights = {}

    def forward(buffer, b, n, h):
        for way, (to, sign, hops) in enumerate(ways):
            if (way, b, n, h - 1) in flights:
                flights[way, b, n, h - 1].wait_recv()
            if h < hops:
                slot = lax.rem(e + sign * h + ring, ring)
                part = buffer.at[slot, pl.ds(n * 16, 16)]
                index = ((b * 4 + n) * 2 + way) * steps + h
                copy = pltpu.make_async_remote_copy(
                    src_ref=part,
                    dst_ref=part,
                    send_sem=z_send.at[index],
                    recv_sem=z_recv.at[index],
                    device_id={"env": to},
                    device_id_type=MESH,
                )
                copy.start()
                flights[way, b, n, h] = copy

    psi_parts = hl.shape[1] // 16
    right_parts = rg.shape[1] // 16
    for n in range(right_parts):
        forward(rg, 1, n, 0)

    for load in loads[2:5]:
        load.wait()
    s, r, w = ids[0], ids[1], ids[2]
    pk_ref[...] = (
        w * 4 + (s >> 3)
        + ((r * (rt_ref.shape[0] // 128) + (w >> 3)) << 8)
        + (((w - s) & 7) << 16)
        + ((w & 7) << 20)
    )

    for copy in spread:
        copy.wait_recv()
    back = got[...].astype(F32).reshape(groups * per, 128).T
    hl[e] = back[: 2 * rows].astype(BF16)

    for h in range(steps + 1):
        for n in range(psi_parts):
            if h < steps:
                forward(hl, 0, n, h)
        if h < steps:
            for n in range(right_parts):
                forward(rg, 1, n, h + 1)

    padded = rg.shape[1]
    out_row = lax.broadcasted_iota(jnp.int32, (rt_ref.shape[0], ring * padded), 0)
    in_row = lax.broadcasted_iota(jnp.int32, (rt_ref.shape[0], ring * padded), 1)
    same = (out_row // ring == in_row % padded) & (out_row % ring == in_row // padded) & (out_row < terms * ring)
    order = jnp.where(same, 1.0, 0.0).astype(BF16)
    rt_ref[...] = jnp.dot(order, rg[...].reshape(ring * padded, cols), preferred_element_type=F32).astype(BF16)

    loads[5].wait()
    for n in range(psi_parts):
        forward(hl, 0, n, steps)
    block = cols // 2
    lanes = q_ref.shape[3]
    lhs = left_ref[...].reshape(terms * rows, cols)
    for half in range(2):
        x_high = hl[:, :rows, half * block : (half + 1) * block].reshape(ring * rows, block)
        x_low = hl[:, rows:, half * block : (half + 1) * block].reshape(ring * rows, block)
        q = jnp.dot(lhs, x_high, preferred_element_type=F32) + jnp.dot(lhs, x_low, preferred_element_type=F32)
        for part in range(block // lanes):
            q_ref[:, half * (block // lanes) + part] = q[:, part * lanes : (part + 1) * lanes].reshape(
                terms, rows, lanes
            )

    for copy in spread:
        copy.wait_send()
    for copy in flights.values():
        copy.wait_send()


def combine_kernel(unroll, q_ref, pk_ref, b0_ref, b1_ref):
    tasks = pk_ref.shape[0] * pk_ref.shape[1]
    lanes = q_ref.shape[-1]
    per = lanes // 8
    b0_ref[...] = jnp.zeros_like(b0_ref)
    b1_ref[...] = jnp.zeros_like(b1_ref)
    shape = q_ref.shape[1:]
    group = lax.broadcasted_iota(jnp.int32, shape, 2) // per

    def step(n, carry):
        moved = []
        for u in range(unroll):
            t = n * unroll + u
            word = pk_ref[t // 128, t % 128]
            block = q_ref[word & 255].reshape(shape[0] * shape[1], lanes)
            block = pltpu.roll(block, ((word >> 16) & 15) * per, axis=1).reshape(shape)
            moved.append(((word >> 8) & 255, jnp.where(group == (word >> 20), block, 0.0)))
        for u, (place, block) in enumerate(moved):
            b_ref = (b0_ref, b1_ref)[u % 2]
            b_ref[place] = b_ref[place] + block
        return carry

    lax.fori_loop(0, tasks // unroll, step, 0)


def scatter_kernel(b0_ref, b1_ref, rt_ref, o_ref, mine, pair, acc, xa, yb, ca, cb, ya, xb, send, recv):
    g = lax.axis_index("sec")
    core = lax.rem(g, 2)
    x = lax.rem(g // 2, 4)
    y = g // 8
    sibling = g + 1 - 2 * core
    half = o_ref.shape[1] // 2
    tiles = b0_ref.shape[2]

    def x_peer(d):
        return (y * 4 + lax.rem(x + d, 4)) * 2 + core

    def y_peer(d):
        return (lax.rem(y + d, 4) * 4 + x) * 2 + core

    barrier = pltpu.get_barrier_semaphore()
    peers = [sibling] + [x_peer(d) for d in (1, 2, 3)] + [y_peer(d) for d in (1, 2, 3)]
    for to in peers:
        pl.semaphore_signal(barrier, inc=1, device_id={"sec": to}, device_id_type=MESH)

    def product(parity, k):
        at = pl.ds(k * half, half)
        b = jnp.concatenate(
            [b0_ref[:, parity, n, at] + b1_ref[:, parity, n, at] for n in range(tiles)], axis=2
        )
        b = b.reshape(b.shape[0] * half, b.shape[2])
        top = b.astype(BF16)
        rest = (b - top.astype(F32)).astype(BF16)
        return jnp.dot(top, rt_ref[...], preferred_element_type=F32) + jnp.dot(
            rest, rt_ref[...], preferred_element_type=F32
        )

    def copy(src, dst, index, to):
        made = pltpu.make_async_remote_copy(
            src_ref=src,
            dst_ref=dst,
            send_sem=send.at[index],
            recv_sem=recv.at[index],
            device_id={"sec": to},
            device_id_type=MESH,
        )
        made.start()
        return made

    first, second, third = [], [], []
    for k in range(2):
        mine[k] = product(1 - core, k).reshape(mine.shape[1:])
        if k == 0:
            pl.semaphore_wait(barrier, len(peers))
        first.append(copy(mine.at[k], pair.at[k], k, sibling))
    for k in range(2):
        own = product(core, k).reshape(acc.shape[1:])
        first[k].wait_recv()
        acc[k] = own + pair[k].reshape(acc.shape[1:])
        for d in (2, 1, 3):
            index = 2 + k * 3 + d - 1
            if k == 0:
                second.append(copy(acc.at[0, :, lax.rem(x + d, 4)], xa.at[d - 1], index, x_peer(d)))
            else:
                second.append(copy(acc.at[1, lax.rem(y + d, 4)], yb.at[d - 1], index, y_peer(d)))
    for k in range(2):
        for d in (1, 2, 3):
            second[k * 3 + d - 1].wait_recv()
        if k == 0:
            ca[...] = acc[0, :, x] + xa[0] + xa[1] + xa[2]
        else:
            cb[...] = acc[1, y] + yb[0] + yb[1] + yb[2]
        for d in (2, 1, 3):
            index = 8 + k * 3 + d - 1
            if k == 0:
                third.append(copy(ca.at[lax.rem(y + d, 4)], ya.at[d - 1], index, y_peer(d)))
            else:
                third.append(copy(cb.at[lax.rem(x + d, 4)], xb.at[d - 1], index, x_peer(d)))
    for k in range(2):
        for d in (1, 2, 3):
            third[k * 3 + d - 1].wait_recv()
        if k == 0:
            o_ref[0, :half] = ca[y] + ya[0] + ya[1] + ya[2]
        else:
            o_ref[0, half:] = cb[x] + xb[0] + xb[1] + xb[2]
    for made in first + second + third:
        made.wait_send()


def body(wavefunction, left_env, right_env, task_in, task_out, task_term):
    groups = lax.axis_size("sec")
    ring = lax.axis_size("env")
    _, rows, cols = wavefunction.shape
    terms = left_env.shape[0]
    per = cols // groups
    padded = -(-terms // 16) * 16
    tiles = -(-terms // 8)
    limit = 40 * 2**20
    sems = pltpu.SemaphoreType.DMA
    ids = (task_in.shape[0] // 128, 128)
    hbm = pl.BlockSpec(memory_space=pltpu.HBM)

    q, rt, packed = pl.pallas_call(
        functools.partial(gather_kernel, groups, ring),
        out_shape=(
            jax.ShapeDtypeStruct((terms, groups // 8, rows, 128), F32),
            jax.ShapeDtypeStruct((tiles * 128, cols), BF16),
            jax.ShapeDtypeStruct(ids, jnp.int32),
        ),
        in_specs=[hbm] * 6,
        out_specs=(vmem(), vmem(), vmem()),
        scratch_shapes=[
            pltpu.VMEM(wavefunction.shape, F32),
            pltpu.VMEM(left_env.shape, BF16),
            pltpu.VMEM(right_env.shape, BF16),
            pltpu.VMEM((3, *ids), jnp.int32),
            pltpu.VMEM((cols, 128), F32),
            pltpu.VMEM((groups, per, 128), BF16),
            pltpu.VMEM((groups, per, 128), BF16),
            pltpu.VMEM((ring, 2 * rows, cols), BF16),
            pltpu.VMEM((ring, padded, cols), BF16),
            pltpu.VMEM((padded, cols), F32),
            sems((groups,)),
            sems((groups,)),
            sems((8 * ring,)),
            sems((8 * ring,)),
            sems((6,)),
        ],
        compiler_params=pltpu.CompilerParams(collective_id=0, has_side_effects=True, vmem_limit_bytes=limit),
        name="gather_psi",
    )(*(
        pltpu.with_memory_space_constraint(a, pltpu.HBM)
        for a in (wavefunction, left_env, right_env, task_in.reshape(ids), task_out.reshape(ids), task_term.reshape(ids))
    ))

    sums = jax.ShapeDtypeStruct((groups * tiles, rows // 8, 8, 128), F32)
    even, odd = pl.pallas_call(
        functools.partial(combine_kernel, 16),
        out_shape=(sums, sums),
        in_specs=[vmem(), pl.BlockSpec(memory_space=pltpu.SMEM)],
        out_specs=(vmem(), vmem()),
        compiler_params=pltpu.CompilerParams(vmem_limit_bytes=limit),
        name="combine_tasks",
    )(q.reshape(terms * (groups // 8), rows // 8, 8, 128), packed)

    half = rows // 2
    split = (groups // 2, 2, tiles, rows, 128)
    return pl.pallas_call(
        scatter_kernel,
        out_shape=jax.ShapeDtypeStruct((1, rows, cols), F32),
        in_specs=[vmem()] * 3,
        out_specs=vmem(),
        scratch_shapes=[
            pltpu.VMEM((2, 16, half, cols), F32),
            pltpu.VMEM((2, 16, half, cols), F32),
            pltpu.VMEM((2, 4, 4, half, cols), F32),
            pltpu.VMEM((3, 4, half, cols), F32),
            pltpu.VMEM((3, 4, half, cols), F32),
            pltpu.VMEM((4, half, cols), F32),
            pltpu.VMEM((4, half, cols), F32),
            pltpu.VMEM((3, half, cols), F32),
            pltpu.VMEM((3, half, cols), F32),
            sems((14,)),
            sems((14,)),
        ],
        compiler_params=pltpu.CompilerParams(collective_id=1, has_side_effects=True, vmem_limit_bytes=limit),
        name="scatter_sums",
    )(even.reshape(split), odd.reshape(split), rt)


def solution(mesh):
    placed = (P("sec", "env", None), P(None, "env", None), P(None, "env", None), P(), P(), P())
    return jax.shard_map(
        body, mesh=mesh, in_specs=placed, out_specs=P("sec", "env", None), check_vma=False
    )
```

```python
import functools

import jax
import jax.numpy as jnp
from jax import lax
from jax.experimental import pallas as pl
from jax.experimental.pallas import tpu as pltpu
from jax.sharding import PartitionSpec as P

MESH = pl.DeviceIdType.MESH
F32 = jnp.float32
BF16 = jnp.bfloat16


def vmem():
    return pl.BlockSpec(memory_space=pltpu.VMEM)


def gather_kernel(groups, ring, psi_hbm, left_hbm, right_hbm, in_hbm, out_hbm, term_hbm, q_ref, rt_ref, pk_ref,
                  psi_ref, left_ref, right_ref, ids, t_scr, send_buf, got, hl, rg, rg_last, rrow,
                  a_send, a_recv, z_send, z_recv, local):
    g = lax.axis_index("sec")
    e = lax.axis_index("env")
    terms = left_ref.shape[0]
    rows = psi_ref.shape[1]
    cols = psi_ref.shape[2]
    per = cols // groups
    right = lax.rem(e + 1, ring)
    left = lax.rem(e + ring - 1, ring)
    jump = ring // 4
    far_right = lax.rem(e + jump, ring)
    far_left = lax.rem(e + ring - jump, ring)

    loads = [
        pltpu.make_async_copy(src, dst, local.at[n])
        for n, (src, dst) in enumerate(
            (
                (psi_hbm, psi_ref),
                (right_hbm, right_ref),
                (in_hbm, ids.at[0]),
                (out_hbm, ids.at[1]),
                (term_hbm, ids.at[2]),
                (left_hbm, left_ref),
            )
        )
    ]
    for load in loads:
        load.start()

    barrier = pltpu.get_barrier_semaphore()
    for d in range(1, groups):
        pl.semaphore_signal(barrier, inc=1, device_id={"sec": lax.rem(g + d, groups)}, device_id_type=MESH)
    for to in (left, right, far_left, far_right):
        pl.semaphore_signal(barrier, inc=1, device_id={"env": to}, device_id_type=MESH)

    loads[0].wait()
    psi = psi_ref[0]
    high = psi.astype(BF16)
    low = (psi - high.astype(F32)).astype(BF16)
    stacked = jnp.concatenate(
        [high.astype(F32), low.astype(F32), jnp.zeros((128 - 2 * rows, cols), F32)], axis=0
    )
    t_scr[...] = stacked.T
    for p in range(groups):
        send_buf[p] = t_scr[pl.ds(p, per, stride=groups), :].astype(BF16)

    pl.semaphore_wait(barrier, groups + 3)

    spread = []
    for d in range(1, groups):
        to = lax.rem(g + d, groups)
        copy = pltpu.make_async_remote_copy(
            src_ref=send_buf.at[to],
            dst_ref=got.at[g],
            send_sem=a_send.at[d],
            recv_sem=a_recv.at[d],
            device_id={"sec": to},
            device_id_type=MESH,
        )
        copy.start()
        spread.append(copy)
    got[g] = send_buf[g]

    main = rg.shape[1]
    loads[1].wait()
    rrow[...] = jnp.zeros_like(rrow)
    pick = lax.broadcasted_iota(jnp.int32, (rows, cols), 0) == g
    for w in range(terms):
        row = jnp.sum(jnp.where(pick, right_ref[w].astype(F32), 0.0), axis=0, keepdims=True)
        rrow[pl.ds(w, 1), :] = row
    rg[e] = rrow[:main].astype(BF16)

    steps = ring // 2
    flights = {}
    used = []

    def forward(chain, h):
        key, buffer, hops, place = chain
        if (key, h - 1) in flights:
            flights[key, h - 1].wait_recv()
        if h < hops:
            off, to = place(h)
            part = buffer.at[lax.rem(e + off + ring, ring)]
            index = len(used)
            used.append(index)
            copy = pltpu.make_async_remote_copy(
                src_ref=part,
                dst_ref=part,
                send_sem=z_send.at[index],
                recv_sem=z_recv.at[index],
                device_id={"env": to},
                device_id_type=MESH,
            )
            copy.start()
            flights[key, h] = copy

    def chains(key, buffer):
        return (
            (key + "br", buffer, steps - jump + 1, lambda h: (1 - jump - h, right) if h else (0, far_right)),
            (key + "bl", buffer, steps - jump, lambda h: (jump - 1 + h, left) if h else (0, far_left)),
            (key + "ar", buffer, jump - 1, lambda h: (-h, right)),
            (key + "al", buffer, jump - 1, lambda h: (h, left)),
        )

    psi_chains = chains("p", hl) + chains("t", rg_last)
    right_chains = chains("m", rg)
    last_step = steps - jump + 1

    def move(group, h):
        for chain in group:
            forward(chain, h)

    move(right_chains, 0)

    for load in loads[2:5]:
        load.wait()
    s, r, w = ids[0], ids[1], ids[2]
    pk_ref[...] = (
        w * 4 + (s >> 3)
        + ((r * (rt_ref.shape[0] // 128) + (w >> 3)) << 8)
        + (((w - s) & 7) << 16)
        + ((w & 7) << 20)
    )

    for copy in spread:
        copy.wait_recv()
    back = got[...].astype(F32).reshape(groups * per, 128).T
    block = back[:rows] + back[rows : 2 * rows]
    most = jnp.max(jnp.abs(block), axis=0, keepdims=True)
    scale = (most * (1.01 / 32767)).astype(BF16).astype(F32)
    inverse = jnp.where(scale > 0, 1.0 / jnp.where(scale > 0, scale, 1.0), 0.0)
    hl[e] = jnp.round(block * inverse).astype(jnp.int32).astype(jnp.int16)
    wide = cols // 128
    used_rows = wide * (terms - main)
    tail = jnp.concatenate(
        [rrow[pl.ds(main + n // wide, 1), (n % wide) * 128 : (n % wide + 1) * 128] for n in range(used_rows)]
        + [scale[:, n * 128 : (n + 1) * 128] for n in range(wide)]
        + [jnp.zeros((16 - used_rows - wide, 128), F32)],
        axis=0,
    )
    rg_last[e] = tail.astype(BF16)

    for h in range(last_step):
        move(psi_chains, h)
        move(right_chains, h + 1)

    out_row = lax.broadcasted_iota(jnp.int32, (main * ring, ring * main), 0)
    in_row = lax.broadcasted_iota(jnp.int32, (main * ring, ring * main), 1)
    same = (out_row // ring == in_row % main) & (out_row % ring == in_row // main)
    order = jnp.where(same, 1.0, 0.0).astype(BF16)
    rt_ref[: main * ring] = jnp.dot(
        order, rg[...].reshape(ring * main, cols), preferred_element_type=F32
    ).astype(BF16)

    move(psi_chains, last_step)
    loads[5].wait()
    lanes = q_ref.shape[3]
    lhs = left_ref[...].reshape(terms * rows, cols)
    block = 2 * lanes
    for half in range(cols // block):
        high, low = [], []
        for k in range(ring):
            tail = rg_last[k].astype(F32)
            scale = jnp.concatenate(
                [tail[used_rows + 2 * half + n : used_rows + 2 * half + n + 1] for n in range(2)], axis=1
            )
            x = hl[k, :, half * block : (half + 1) * block].astype(jnp.int32).astype(F32) * scale
            high.append(x.astype(BF16))
            low.append((x - high[-1].astype(F32)).astype(BF16))
        q = jnp.dot(lhs, jnp.concatenate(high, axis=0), preferred_element_type=F32) + jnp.dot(
            lhs, jnp.concatenate(low, axis=0), preferred_element_type=F32
        )
        for part in range(2):
            q_ref[:, half * 2 + part] = q[:, part * lanes : (part + 1) * lanes].reshape(terms, rows, lanes)

    last = rt_ref.shape[0] - main * ring
    out_row = lax.broadcasted_iota(jnp.int32, (last, ring * 16), 0)
    in_row = lax.broadcasted_iota(jnp.int32, (last, ring * 16), 1)
    for n in range(wide):
        same = (out_row % ring == in_row // 16) & ((out_row // ring) * wide + n == in_row % 16) & (in_row % 16 < used_rows)
        order = jnp.where(same, 1.0, 0.0).astype(BF16)
        rt_ref[main * ring :, n * 128 : (n + 1) * 128] = jnp.dot(
            order, rg_last[...].reshape(ring * 16, 128), preferred_element_type=F32
        ).astype(BF16)

    for copy in spread:
        copy.wait_send()
    for copy in flights.values():
        copy.wait_send()


def combine_kernel(unroll, q_ref, pk_ref, b0_ref, b1_ref):
    tasks = pk_ref.shape[0] * pk_ref.shape[1]
    lanes = q_ref.shape[-1]
    per = lanes // 8
    b0_ref[...] = jnp.zeros_like(b0_ref)
    b1_ref[...] = jnp.zeros_like(b1_ref)
    shape = q_ref.shape[1:]
    group = lax.broadcasted_iota(jnp.int32, shape, 2) // per

    def step(n, carry):
        moved = []
        for u in range(unroll):
            t = n * unroll + u
            word = pk_ref[t // 128, t % 128]
            block = q_ref[word & 255].reshape(shape[0] * shape[1], lanes)
            block = pltpu.roll(block, ((word >> 16) & 15) * per, axis=1).reshape(shape)
            moved.append(((word >> 8) & 255, jnp.where(group == (word >> 20), block, 0.0)))
        for u, (place, block) in enumerate(moved):
            b_ref = (b0_ref, b1_ref)[u % 2]
            b_ref[place] = b_ref[place] + block
        return carry

    lax.fori_loop(0, tasks // unroll, step, 0)


def scatter_kernel(b0_ref, b1_ref, rt_ref, o_ref, mine, pair, acc, xa, yb, ca, cb, ya, xb, send, recv):
    g = lax.axis_index("sec")
    core = lax.rem(g, 2)
    x = lax.rem(g // 2, 4)
    y = g // 8
    sibling = g + 1 - 2 * core
    half = o_ref.shape[1] // 2
    tiles = b0_ref.shape[2]

    def x_peer(d):
        return (y * 4 + lax.rem(x + d, 4)) * 2 + core

    def y_peer(d):
        return (lax.rem(y + d, 4) * 4 + x) * 2 + core

    barrier = pltpu.get_barrier_semaphore()
    peers = [sibling] + [x_peer(d) for d in (1, 2, 3)] + [y_peer(d) for d in (1, 2, 3)]
    for to in peers:
        pl.semaphore_signal(barrier, inc=1, device_id={"sec": to}, device_id_type=MESH)

    def product(parity, k):
        at = pl.ds(k * half, half)
        b = jnp.concatenate(
            [b0_ref[:, parity, n, at] + b1_ref[:, parity, n, at] for n in range(tiles)], axis=2
        )
        b = b.reshape(b.shape[0] * half, b.shape[2])
        top = b.astype(BF16)
        rest = (b - top.astype(F32)).astype(BF16)
        return jnp.dot(top, rt_ref[...], preferred_element_type=F32) + jnp.dot(
            rest, rt_ref[...], preferred_element_type=F32
        )

    def copy(src, dst, index, to):
        made = pltpu.make_async_remote_copy(
            src_ref=src,
            dst_ref=dst,
            send_sem=send.at[index],
            recv_sem=recv.at[index],
            device_id={"sec": to},
            device_id_type=MESH,
        )
        made.start()
        return made

    first, second, third = [], [], []
    for k in range(2):
        mine[k] = product(1 - core, k).reshape(mine.shape[1:])
        if k == 0:
            pl.semaphore_wait(barrier, len(peers))
        first.append(copy(mine.at[k], pair.at[k], k, sibling))
    for k in range(2):
        own = product(core, k).reshape(acc.shape[1:])
        first[k].wait_recv()
        acc[k] = own + pair[k].reshape(acc.shape[1:])
        for d in (2, 1, 3):
            index = 2 + k * 3 + d - 1
            if k == 0:
                second.append(copy(acc.at[0, :, lax.rem(x + d, 4)], xa.at[d - 1], index, x_peer(d)))
            else:
                second.append(copy(acc.at[1, lax.rem(y + d, 4)], yb.at[d - 1], index, y_peer(d)))
    for k in range(2):
        for d in (1, 2, 3):
            second[k * 3 + d - 1].wait_recv()
        if k == 0:
            ca[...] = acc[0, :, x] + xa[0] + xa[1] + xa[2]
        else:
            cb[...] = acc[1, y] + yb[0] + yb[1] + yb[2]
        for d in (2, 1, 3):
            index = 8 + k * 3 + d - 1
            if k == 0:
                third.append(copy(ca.at[lax.rem(y + d, 4)], ya.at[d - 1], index, y_peer(d)))
            else:
                third.append(copy(cb.at[lax.rem(x + d, 4)], xb.at[d - 1], index, x_peer(d)))
    for k in range(2):
        for d in (1, 2, 3):
            third[k * 3 + d - 1].wait_recv()
        if k == 0:
            o_ref[0, :half] = ca[y] + ya[0] + ya[1] + ya[2]
        else:
            o_ref[0, half:] = cb[x] + xb[0] + xb[1] + xb[2]
    for made in first + second + third:
        made.wait_send()


def body(wavefunction, left_env, right_env, task_in, task_out, task_term):
    groups = lax.axis_size("sec")
    ring = lax.axis_size("env")
    _, rows, cols = wavefunction.shape
    terms = left_env.shape[0]
    per = cols // groups
    padded = -(-terms // 16) * 16
    tiles = -(-terms // 8)
    limit = 40 * 2**20
    sems = pltpu.SemaphoreType.DMA
    ids = (task_in.shape[0] // 128, 128)
    hbm = pl.BlockSpec(memory_space=pltpu.HBM)

    q, rt, packed = pl.pallas_call(
        functools.partial(gather_kernel, groups, ring),
        out_shape=(
            jax.ShapeDtypeStruct((terms, groups // 8, rows, 128), F32),
            jax.ShapeDtypeStruct((tiles * 128, cols), BF16),
            jax.ShapeDtypeStruct(ids, jnp.int32),
        ),
        in_specs=[hbm] * 6,
        out_specs=(vmem(), vmem(), vmem()),
        scratch_shapes=[
            pltpu.VMEM(wavefunction.shape, F32),
            pltpu.VMEM(left_env.shape, BF16),
            pltpu.VMEM(right_env.shape, BF16),
            pltpu.VMEM((3, *ids), jnp.int32),
            pltpu.VMEM((cols, 128), F32),
            pltpu.VMEM((groups, per, 128), BF16),
            pltpu.VMEM((groups, per, 128), BF16),
            pltpu.VMEM((ring, rows, cols), jnp.int16),
            pltpu.VMEM((ring, terms // 16 * 16, cols), BF16),
            pltpu.VMEM((ring, 16, 128), BF16),
            pltpu.VMEM((padded, cols), F32),
            sems((groups,)),
            sems((groups,)),
            sems((8 * ring,)),
            sems((8 * ring,)),
            sems((6,)),
        ],
        compiler_params=pltpu.CompilerParams(collective_id=0, has_side_effects=True, vmem_limit_bytes=limit),
        name="gather_psi",
    )(*(
        pltpu.with_memory_space_constraint(a, pltpu.HBM)
        for a in (wavefunction, left_env, right_env, task_in.reshape(ids), task_out.reshape(ids), task_term.reshape(ids))
    ))

    sums = jax.ShapeDtypeStruct((groups * tiles, rows // 8, 8, 128), F32)
    even, odd = pl.pallas_call(
        functools.partial(combine_kernel, 16),
        out_shape=(sums, sums),
        in_specs=[vmem(), pl.BlockSpec(memory_space=pltpu.SMEM)],
        out_specs=(vmem(), vmem()),
        compiler_params=pltpu.CompilerParams(vmem_limit_bytes=limit),
        name="combine_tasks",
    )(q.reshape(terms * (groups // 8), rows // 8, 8, 128), packed)

    half = rows // 2
    split = (groups // 2, 2, tiles, rows, 128)
    return pl.pallas_call(
        scatter_kernel,
        out_shape=jax.ShapeDtypeStruct((1, rows, cols), F32),
        in_specs=[vmem()] * 3,
        out_specs=vmem(),
        scratch_shapes=[
            pltpu.VMEM((2, 16, half, cols), F32),
            pltpu.VMEM((2, 16, half, cols), F32),
            pltpu.VMEM((2, 4, 4, half, cols), F32),
            pltpu.VMEM((3, 4, half, cols), F32),
            pltpu.VMEM((3, 4, half, cols), F32),
            pltpu.VMEM((4, half, cols), F32),
            pltpu.VMEM((4, half, cols), F32),
            pltpu.VMEM((3, half, cols), F32),
            pltpu.VMEM((3, half, cols), F32),
            sems((14,)),
            sems((14,)),
        ],
        compiler_params=pltpu.CompilerParams(collective_id=1, has_side_effects=True, vmem_limit_bytes=limit),
        name="scatter_sums",
    )(even.reshape(split), odd.reshape(split), rt)


def solution(mesh):
    placed = (P("sec", "env", None), P(None, "env", None), P(None, "env", None), P(), P(), P())
    return jax.shard_map(
        body, mesh=mesh, in_specs=placed, out_specs=P("sec", "env", None), check_vma=False
    )
```

```python
import functools

import jax
import jax.numpy as jnp
from jax import lax
from jax.experimental import pallas as pl
from jax.experimental.pallas import tpu as pltpu
from jax.sharding import PartitionSpec as P

MESH = pl.DeviceIdType.MESH
F32 = jnp.float32
BF16 = jnp.bfloat16


def vmem():
    return pl.BlockSpec(memory_space=pltpu.VMEM)


def gather_kernel(groups, ring, psi_hbm, left_hbm, right_hbm, in_hbm, out_hbm, term_hbm, q_ref, rt_ref, pk_ref,
                  psi_ref, left_ref, right_ref, ids, t_scr, send_buf, got, hl, rg, rg_last, rrow, xh, xl,
                  a_send, a_recv, z_send, z_recv, local):
    g = lax.axis_index("sec")
    e = lax.axis_index("env")
    terms = left_ref.shape[0]
    rows = psi_ref.shape[1]
    cols = psi_ref.shape[2]
    per = cols // groups
    right = lax.rem(e + 1, ring)
    left = lax.rem(e + ring - 1, ring)
    jump = ring // 4
    far_right = lax.rem(e + jump, ring)
    far_left = lax.rem(e + ring - jump, ring)

    loads = [
        pltpu.make_async_copy(src, dst, local.at[n])
        for n, (src, dst) in enumerate(
            (
                (psi_hbm, psi_ref),
                (right_hbm, right_ref),
                (in_hbm, ids.at[0]),
                (out_hbm, ids.at[1]),
                (term_hbm, ids.at[2]),
                (left_hbm, left_ref),
            )
        )
    ]
    for load in loads:
        load.start()

    barrier = pltpu.get_barrier_semaphore()
    for d in range(1, groups):
        pl.semaphore_signal(barrier, inc=1, device_id={"sec": lax.rem(g + d, groups)}, device_id_type=MESH)
    for to in (left, right, far_left, far_right):
        pl.semaphore_signal(barrier, inc=1, device_id={"env": to}, device_id_type=MESH)

    loads[0].wait()
    psi = psi_ref[0]
    high = psi.astype(BF16)
    low = (psi - high.astype(F32)).astype(BF16)
    stacked = jnp.concatenate(
        [high.astype(F32), low.astype(F32), jnp.zeros((128 - 2 * rows, cols), F32)], axis=0
    )
    t_scr[...] = stacked.T
    for p in range(groups):
        send_buf[p] = t_scr[pl.ds(p, per, stride=groups), :].astype(BF16)

    pl.semaphore_wait(barrier, groups + 3)

    spread = []
    for d in range(1, groups):
        to = lax.rem(g + d, groups)
        copy = pltpu.make_async_remote_copy(
            src_ref=send_buf.at[to],
            dst_ref=got.at[g],
            send_sem=a_send.at[d],
            recv_sem=a_recv.at[d],
            device_id={"sec": to},
            device_id_type=MESH,
        )
        copy.start()
        spread.append(copy)
    got[g] = send_buf[g]

    main = rg.shape[1]
    loads[1].wait()
    rrow[...] = jnp.zeros_like(rrow)
    pick = lax.broadcasted_iota(jnp.int32, (rows, cols), 0) == g
    for w in range(terms):
        row = jnp.sum(jnp.where(pick, right_ref[w].astype(F32), 0.0), axis=0, keepdims=True)
        rrow[pl.ds(w, 1), :] = row
    rg[e] = rrow[:main].astype(BF16)

    steps = ring // 2
    flights = {}
    used = []

    def forward(chain, h):
        key, buffer, hops, place = chain
        if (key, h - 1) in flights:
            flights[key, h - 1].wait_recv()
        if h < hops:
            off, to = place(h)
            part = buffer.at[lax.rem(e + off + ring, ring)]
            index = len(used)
            used.append(index)
            copy = pltpu.make_async_remote_copy(
                src_ref=part,
                dst_ref=part,
                send_sem=z_send.at[index],
                recv_sem=z_recv.at[index],
                device_id={"env": to},
                device_id_type=MESH,
            )
            copy.start()
            flights[key, h] = copy

    def chains(key, buffer):
        return (
            (key + "br", buffer, steps - jump + 1, lambda h: (1 - jump - h, right) if h else (0, far_right)),
            (key + "bl", buffer, steps - jump, lambda h: (jump - 1 + h, left) if h else (0, far_left)),
            (key + "ar", buffer, jump - 1, lambda h: (-h, right)),
            (key + "al", buffer, jump - 1, lambda h: (h, left)),
        )

    psi_chains = chains("p", hl) + chains("t", rg_last)
    right_chains = chains("m", rg)
    last_step = steps - jump + 1

    def move(group, h):
        for chain in group:
            forward(chain, h)

    move(right_chains, 0)

    for load in loads[2:5]:
        load.wait()
    s, r, w = ids[0], ids[1], ids[2]
    pk_ref[...] = (
        w * 4 + (s >> 3)
        + ((r * (rt_ref.shape[0] // 128) + (w >> 3)) << 8)
        + ((((w - s) & 7) * (128 // 8)) << 16)
        + ((w & 7) << 24)
    )

    for copy in spread:
        copy.wait_recv()
    back = got[...].astype(F32).reshape(groups * per, 128).T
    block = back[:rows] + back[rows : 2 * rows]
    most = jnp.max(jnp.abs(block), axis=0, keepdims=True)
    scale = (most * (1.01 / 32767)).astype(BF16).astype(F32)
    inverse = jnp.where(scale > 0, 1.0 / jnp.where(scale > 0, scale, 1.0), 0.0)
    hl[e] = jnp.round(block * inverse).astype(jnp.int32).astype(jnp.int16)
    wide = cols // 128
    used_rows = wide * (terms - main)
    tail = jnp.concatenate(
        [rrow[pl.ds(main + n // wide, 1), (n % wide) * 128 : (n % wide + 1) * 128] for n in range(used_rows)]
        + [scale[:, n * 128 : (n + 1) * 128] for n in range(wide)]
        + [jnp.zeros((16 - used_rows - wide, 128), F32)],
        axis=0,
    )
    rg_last[e] = tail.astype(BF16)

    def unpack(off):
        slot = lax.rem(e + off + ring, ring)
        tail = rg_last[slot].astype(F32)
        scale = jnp.concatenate([tail[used_rows + n : used_rows + n + 1] for n in range(wide)], axis=1)
        x = hl[slot].astype(jnp.int32).astype(F32) * scale
        high = x.astype(BF16)
        xh[slot] = high
        xl[slot] = (x - high.astype(F32)).astype(BF16)

    there = [[0]] + [[] for _ in range(last_step)]
    for h in range(last_step):
        there[h + 1] += [-jump - h] + [jump + h] * (h < steps - jump) + [-1 - h, 1 + h] * (h < jump - 1)
    for h in range(last_step):
        move(psi_chains, h)
        move(right_chains, h + 1)
        for off in there[h]:
            unpack(off)

    out_row = lax.broadcasted_iota(jnp.int32, (main * ring, ring * main), 0)
    in_row = lax.broadcasted_iota(jnp.int32, (main * ring, ring * main), 1)
    same = (out_row // ring == in_row % main) & (out_row % ring == in_row // main)
    order = jnp.where(same, 1.0, 0.0).astype(BF16)
    rt_ref[: main * ring] = jnp.dot(
        order, rg[...].reshape(ring * main, cols), preferred_element_type=F32
    ).astype(BF16)

    move(psi_chains, last_step)
    for off in there[last_step]:
        unpack(off)
    loads[5].wait()
    lanes = q_ref.shape[3]
    lhs = left_ref[...].reshape(terms * rows, cols)
    block = 2 * lanes
    for half in range(cols // block):
        at = slice(half * block, (half + 1) * block)
        q = jnp.dot(lhs, xh[:, :, at].reshape(ring * rows, block), preferred_element_type=F32) + jnp.dot(
            lhs, xl[:, :, at].reshape(ring * rows, block), preferred_element_type=F32
        )
        for part in range(2):
            q_ref[:, half * 2 + part] = q[:, part * lanes : (part + 1) * lanes].reshape(terms, rows, lanes)

    last = rt_ref.shape[0] - main * ring
    out_row = lax.broadcasted_iota(jnp.int32, (last, ring * 16), 0)
    in_row = lax.broadcasted_iota(jnp.int32, (last, ring * 16), 1)
    for n in range(wide):
        same = (out_row % ring == in_row // 16) & ((out_row // ring) * wide + n == in_row % 16) & (in_row % 16 < used_rows)
        order = jnp.where(same, 1.0, 0.0).astype(BF16)
        rt_ref[main * ring :, n * 128 : (n + 1) * 128] = jnp.dot(
            order, rg_last[...].reshape(ring * 16, 128), preferred_element_type=F32
        ).astype(BF16)

    for copy in spread:
        copy.wait_send()
    for copy in flights.values():
        copy.wait_send()


def combine_kernel(unroll, q_ref, pk_ref, b0_ref, b1_ref):
    lanes = q_ref.shape[-1]
    per = lanes // 8
    b0_ref[...] = jnp.zeros_like(b0_ref)
    b1_ref[...] = jnp.zeros_like(b1_ref)
    shape = q_ref.shape[1:]
    group = lax.broadcasted_iota(jnp.int32, shape, 2) // per

    def step(line, n, carry):
        moved = []
        for u in range(unroll):
            word = pk_ref[line, n * unroll + u]
            block = q_ref[word & 255].reshape(shape[0] * shape[1], lanes)
            block = pltpu.roll(block, (word >> 16) & 127, axis=1).reshape(shape)
            moved.append(((word >> 8) & 255, jnp.where(group == (word >> 24), block, 0.0)))
        for u, (place, block) in enumerate(moved):
            b_ref = (b0_ref, b1_ref)[u % 2]
            b_ref[place] = b_ref[place] + block
        return carry

    for line in range(pk_ref.shape[0]):
        lax.fori_loop(0, pk_ref.shape[1] // unroll, functools.partial(step, line), 0)


def scatter_kernel(b0_ref, b1_ref, rt_ref, o_ref, mine, pair, acc, coded, steps, xa, yb, xs, ys, ca, cb, ya, xb, send, recv):
    g = lax.axis_index("sec")
    core = lax.rem(g, 2)
    x = lax.rem(g // 2, 4)
    y = g // 8
    sibling = g + 1 - 2 * core
    half = o_ref.shape[1] // 2
    tiles = b0_ref.shape[2]

    def x_peer(d):
        return (y * 4 + lax.rem(x + d, 4)) * 2 + core

    def y_peer(d):
        return (lax.rem(y + d, 4) * 4 + x) * 2 + core

    barrier = pltpu.get_barrier_semaphore()
    peers = [sibling] + [x_peer(d) for d in (1, 2, 3)] + [y_peer(d) for d in (1, 2, 3)]
    for to in peers:
        pl.semaphore_signal(barrier, inc=1, device_id={"sec": to}, device_id_type=MESH)

    def product(parity, k):
        at = pl.ds(k * half, half)
        b = jnp.concatenate(
            [b0_ref[:, parity, n, at] + b1_ref[:, parity, n, at] for n in range(tiles)], axis=2
        )
        b = b.reshape(b.shape[0] * half, b.shape[2])
        top = b.astype(BF16)
        rest = (b - top.astype(F32)).astype(BF16)
        return jnp.dot(top, rt_ref[...], preferred_element_type=F32) + jnp.dot(
            rest, rt_ref[...], preferred_element_type=F32
        )

    def copy(src, dst, index, to):
        made = pltpu.make_async_remote_copy(
            src_ref=src,
            dst_ref=dst,
            send_sem=send.at[index],
            recv_sem=recv.at[index],
            device_id={"sec": to},
            device_id_type=MESH,
        )
        made.start()
        return made

    steps[...] = jnp.zeros_like(steps)
    first, second, scales, third = [], [], [], []

    def decoded(values, scale):
        return [values[n].astype(jnp.int32).astype(F32) * scale[n : n + 1, :1] for n in range(4)]

    for k in range(2):
        mine[k] = product(1 - core, k).reshape(mine.shape[1:])
        if k == 0:
            pl.semaphore_wait(barrier, len(peers))
        first.append(copy(mine.at[k], pair.at[k], k, sibling))
    for k in range(2):
        own = product(core, k).reshape(acc.shape[1:])
        first[k].wait_recv()
        acc[k] = own + pair[k].reshape(acc.shape[1:])
        for n in range(16):
            part = acc[k, n // 4, n % 4]
            most = jnp.max(jnp.max(jnp.abs(part), axis=0, keepdims=True), axis=1, keepdims=True)
            scale = most * (1.01 / 32767)
            inverse = jnp.where(scale > 0, 1.0 / jnp.where(scale > 0, scale, 1.0), 0.0)
            coded[k, n // 4, n % 4] = jnp.round(part * inverse).astype(jnp.int32).astype(jnp.int16)
            wide = jnp.broadcast_to(scale, (1, 128))
            if k == 0:
                steps[k, n % 4, pl.ds(n // 4, 1), :] = wide
            else:
                steps[k, n // 4, pl.ds(n % 4, 1), :] = wide
        for d in (2, 1, 3):
            index = 2 + k * 3 + d - 1
            if k == 0:
                to = lax.rem(x + d, 4)
                second.append(copy(coded.at[0, :, to], xa.at[d - 1], index, x_peer(d)))
                scales.append(copy(steps.at[0, to], xs.at[d - 1], index + 12, x_peer(d)))
            else:
                to = lax.rem(y + d, 4)
                second.append(copy(coded.at[1, to], yb.at[d - 1], index, y_peer(d)))
                scales.append(copy(steps.at[1, to], ys.at[d - 1], index + 12, y_peer(d)))
    for k in range(2):
        for d in (1, 2, 3):
            second[k * 3 + d - 1].wait_recv()
            scales[k * 3 + d - 1].wait_recv()
        if k == 0:
            parts = [decoded(xa[d], xs[d]) for d in range(3)]
            for n in range(4):
                ca[n] = acc[0, n, x] + parts[0][n] + parts[1][n] + parts[2][n]
        else:
            parts = [decoded(yb[d], ys[d]) for d in range(3)]
            for n in range(4):
                cb[n] = acc[1, y, n] + parts[0][n] + parts[1][n] + parts[2][n]
        for d in (2, 1, 3):
            index = 8 + k * 3 + d - 1
            if k == 0:
                third.append(copy(ca.at[lax.rem(y + d, 4)], ya.at[d - 1], index, y_peer(d)))
            else:
                third.append(copy(cb.at[lax.rem(x + d, 4)], xb.at[d - 1], index, x_peer(d)))
    for k in range(2):
        for d in (1, 2, 3):
            third[k * 3 + d - 1].wait_recv()
        if k == 0:
            o_ref[0, :half] = ca[y] + ya[0] + ya[1] + ya[2]
        else:
            o_ref[0, half:] = cb[x] + xb[0] + xb[1] + xb[2]
    for made in first + second + scales + third:
        made.wait_send()


def body(wavefunction, left_env, right_env, task_in, task_out, task_term):
    groups = lax.axis_size("sec")
    ring = lax.axis_size("env")
    _, rows, cols = wavefunction.shape
    terms = left_env.shape[0]
    per = cols // groups
    padded = -(-terms // 16) * 16
    tiles = -(-terms // 8)
    limit = 40 * 2**20
    sems = pltpu.SemaphoreType.DMA
    ids = (task_in.shape[0] // 128, 128)
    hbm = pl.BlockSpec(memory_space=pltpu.HBM)

    q, rt, packed = pl.pallas_call(
        functools.partial(gather_kernel, groups, ring),
        out_shape=(
            jax.ShapeDtypeStruct((terms, groups // 8, rows, 128), F32),
            jax.ShapeDtypeStruct((tiles * 128, cols), BF16),
            jax.ShapeDtypeStruct(ids, jnp.int32),
        ),
        in_specs=[hbm] * 6,
        out_specs=(vmem(), vmem(), vmem()),
        scratch_shapes=[
            pltpu.VMEM(wavefunction.shape, F32),
            pltpu.VMEM(left_env.shape, BF16),
            pltpu.VMEM(right_env.shape, BF16),
            pltpu.VMEM((3, *ids), jnp.int32),
            pltpu.VMEM((cols, 128), F32),
            pltpu.VMEM((groups, per, 128), BF16),
            pltpu.VMEM((groups, per, 128), BF16),
            pltpu.VMEM((ring, rows, cols), jnp.int16),
            pltpu.VMEM((ring, terms // 16 * 16, cols), BF16),
            pltpu.VMEM((ring, 16, 128), BF16),
            pltpu.VMEM((padded, cols), F32),
            pltpu.VMEM((ring, rows, cols), BF16),
            pltpu.VMEM((ring, rows, cols), BF16),
            sems((groups,)),
            sems((groups,)),
            sems((8 * ring,)),
            sems((8 * ring,)),
            sems((6,)),
        ],
        compiler_params=pltpu.CompilerParams(collective_id=0, has_side_effects=True, vmem_limit_bytes=limit),
        name="gather_psi",
    )(*(
        pltpu.with_memory_space_constraint(a, pltpu.HBM)
        for a in (wavefunction, left_env, right_env, task_in.reshape(ids), task_out.reshape(ids), task_term.reshape(ids))
    ))

    sums = jax.ShapeDtypeStruct((groups * tiles, rows // 8, 8, 128), F32)
    even, odd = pl.pallas_call(
        functools.partial(combine_kernel, 16),
        out_shape=(sums, sums),
        in_specs=[vmem(), pl.BlockSpec(memory_space=pltpu.SMEM)],
        out_specs=(vmem(), vmem()),
        compiler_params=pltpu.CompilerParams(vmem_limit_bytes=limit),
        name="combine_tasks",
    )(q.reshape(terms * (groups // 8), rows // 8, 8, 128), packed)

    half = rows // 2
    split = (groups // 2, 2, tiles, rows, 128)
    return pl.pallas_call(
        scatter_kernel,
        out_shape=jax.ShapeDtypeStruct((1, rows, cols), F32),
        in_specs=[vmem()] * 3,
        out_specs=vmem(),
        scratch_shapes=[
            pltpu.VMEM((2, 16, half, cols), F32),
            pltpu.VMEM((2, 16, half, cols), F32),
            pltpu.VMEM((2, 4, 4, half, cols), F32),
            pltpu.VMEM((2, 4, 4, half, cols), jnp.int16),
            pltpu.VMEM((2, 4, 8, 128), F32),
            pltpu.VMEM((3, 4, half, cols), jnp.int16),
            pltpu.VMEM((3, 4, half, cols), jnp.int16),
            pltpu.VMEM((3, 8, 128), F32),
            pltpu.VMEM((3, 8, 128), F32),
            pltpu.VMEM((4, half, cols), F32),
            pltpu.VMEM((4, half, cols), F32),
            pltpu.VMEM((3, half, cols), F32),
            pltpu.VMEM((3, half, cols), F32),
            sems((20,)),
            sems((20,)),
        ],
        compiler_params=pltpu.CompilerParams(collective_id=1, has_side_effects=True, vmem_limit_bytes=limit),
        name="scatter_sums",
    )(even.reshape(split), odd.reshape(split), rt)


def solution(mesh):
    placed = (P("sec", "env", None), P(None, "env", None), P(None, "env", None), P(), P(), P())
    return jax.shard_map(
        body, mesh=mesh, in_specs=placed, out_specs=P("sec", "env", None), check_vma=False
    )
```

```python
import functools

import jax
import jax.numpy as jnp
from jax import lax
from jax.experimental import pallas as pl
from jax.experimental.pallas import tpu as pltpu
from jax.sharding import PartitionSpec as P

MESH = pl.DeviceIdType.MESH
F32 = jnp.float32
BF16 = jnp.bfloat16


def vmem():
    return pl.BlockSpec(memory_space=pltpu.VMEM)


def gather_kernel(groups, ring, psi_hbm, left_hbm, right_hbm, in_hbm, out_hbm, term_hbm, q_ref, rt_ref, pk_ref,
                  psi_ref, left_ref, right_ref, ids, t_scr, send_buf, got, hl, rg, rg_last, rrow, xh, xl,
                  a_send, a_recv, z_send, z_recv, local):
    g = lax.axis_index("sec")
    e = lax.axis_index("env")
    terms = left_ref.shape[0]
    rows = psi_ref.shape[1]
    cols = psi_ref.shape[2]
    per = cols // groups
    right = lax.rem(e + 1, ring)
    left = lax.rem(e + ring - 1, ring)
    steps = ring // 2
    psi_starts = (1, 5)
    right_starts = (1, 5)
    leaps = sorted({1, *psi_starts, *right_starts})

    loads = [
        pltpu.make_async_copy(src, dst, local.at[n])
        for n, (src, dst) in enumerate(
            (
                (psi_hbm, psi_ref),
                (right_hbm, right_ref),
                (in_hbm, ids.at[0]),
                (out_hbm, ids.at[1]),
                (term_hbm, ids.at[2]),
                (left_hbm, left_ref),
            )
        )
    ]
    for load in loads:
        load.start()

    barrier = pltpu.get_barrier_semaphore()
    for d in range(1, groups):
        pl.semaphore_signal(barrier, inc=1, device_id={"sec": lax.rem(g + d, groups)}, device_id_type=MESH)
    for to in [lax.rem(e + leap, ring) for leap in (*leaps, *(ring - leap for leap in leaps))]:
        pl.semaphore_signal(barrier, inc=1, device_id={"env": to}, device_id_type=MESH)

    loads[0].wait()
    psi = psi_ref[0]
    high = psi.astype(BF16)
    low = (psi - high.astype(F32)).astype(BF16)
    stacked = jnp.concatenate(
        [high.astype(F32), low.astype(F32), jnp.zeros((128 - 2 * rows, cols), F32)], axis=0
    )
    t_scr[...] = stacked.T
    for p in range(groups):
        send_buf[p] = t_scr[pl.ds(p, per, stride=groups), :].astype(BF16)

    pl.semaphore_wait(barrier, groups - 1 + 2 * len(leaps))

    spread = []
    for d in range(1, groups):
        to = lax.rem(g + d, groups)
        copy = pltpu.make_async_remote_copy(
            src_ref=send_buf.at[to],
            dst_ref=got.at[g],
            send_sem=a_send.at[d],
            recv_sem=a_recv.at[d],
            device_id={"sec": to},
            device_id_type=MESH,
        )
        copy.start()
        spread.append(copy)
    got[g] = send_buf[g]

    main = rg.shape[1]
    loads[1].wait()
    rrow[...] = jnp.zeros_like(rrow)
    pick = lax.broadcasted_iota(jnp.int32, (rows, cols), 0) == g
    for w in range(terms):
        row = jnp.sum(jnp.where(pick, right_ref[w].astype(F32), 0.0), axis=0, keepdims=True)
        rrow[pl.ds(w, 1), :] = row
    rg[e] = rrow[:main].astype(BF16)

    flights = {}
    used = []

    def forward(chain, h):
        key, buffer, hops, place, _ = chain
        if (key, h - 1) in flights:
            flights[key, h - 1].wait_recv()
        if h < hops:
            off, to = place(h)
            part = buffer.at[lax.rem(e + off + ring, ring)]
            index = len(used)
            used.append(index)
            copy = pltpu.make_async_remote_copy(
                src_ref=part,
                dst_ref=part,
                send_sem=z_send.at[index],
                recv_sem=z_recv.at[index],
                device_id={"env": to},
                device_id_type=MESH,
            )
            copy.start()
            flights[key, h] = copy

    def chains(key, buffer, starts):
        made = []
        for n in range(len(starts) - 1, -1, -1):
            o = starts[n]
            for sign, end in ((1, steps + 1), (-1, steps)):
                stop = min(starts[n + 1], end) if n + 1 < len(starts) else end
                beside = right if sign > 0 else left
                seed = lax.rem(e + sign * o + ring, ring)
                place = functools.partial(
                    lambda sign, o, seed, beside, h: (-sign * (o + h - 1), beside) if h else (0, seed),
                    sign, o, seed, beside,
                )
                made.append((key + str(sign * o), buffer, stop - o, place, [-sign * k for k in range(o, stop)]))
        return made

    psi_chains = chains("p", hl, psi_starts)
    tail_chains = chains("t", rg_last, psi_starts)
    right_chains = chains("m", rg, right_starts)
    last_step = max(chain[2] for chain in psi_chains)
    right_last = max(chain[2] for chain in right_chains)

    def move(group, h):
        for chain in group:
            forward(chain, h)

    move(right_chains, 0)

    for load in loads[2:5]:
        load.wait()
    s, r, w = ids[0], ids[1], ids[2]
    pk_ref[...] = (
        w * 4 + (s >> 3)
        + ((r * (rt_ref.shape[0] // 128) + (w >> 3)) << 8)
        + ((((w - s) & 7) * (128 // 8)) << 16)
        + ((w & 7) << 24)
    )

    for copy in spread:
        copy.wait_recv()
    back = got[...].astype(F32).reshape(groups * per, 128).T
    block = back[:rows] + back[rows : 2 * rows]
    most = jnp.max(jnp.abs(block), axis=0, keepdims=True)
    scale = (most * (1.01 / 32767)).astype(BF16).astype(F32)
    inverse = jnp.where(scale > 0, 1.0 / jnp.where(scale > 0, scale, 1.0), 0.0)
    hl[e] = jnp.round(block * inverse).astype(jnp.int32).astype(jnp.int16)
    wide = cols // 128
    used_rows = wide * (terms - main)
    tail = jnp.concatenate(
        [rrow[pl.ds(main + n // wide, 1), (n % wide) * 128 : (n % wide + 1) * 128] for n in range(used_rows)]
        + [scale[:, n * 128 : (n + 1) * 128] for n in range(wide)]
        + [jnp.zeros((16 - used_rows - wide, 128), F32)],
        axis=0,
    )
    rg_last[e] = tail.astype(BF16)

    def unpack(off):
        slot = lax.rem(e + off + ring, ring)
        tail = rg_last[slot].astype(F32)
        scale = jnp.concatenate([tail[used_rows + n : used_rows + n + 1] for n in range(wide)], axis=1)
        x = hl[slot].astype(jnp.int32).astype(F32) * scale
        high = x.astype(BF16)
        xh[slot] = high
        xl[slot] = (x - high.astype(F32)).astype(BF16)

    there = [[0]] + [[] for _ in range(last_step)]
    for chain in psi_chains:
        for h, off in enumerate(chain[4]):
            there[h + 1].append(off)
    for h in range(max(last_step, right_last)):
        if h < last_step:
            move(psi_chains + tail_chains, h)
        move(right_chains, h + 1)
        if h < last_step:
            for off in there[h]:
                unpack(off)
        if h == 0:
            for copy in spread:
                copy.wait_send()
        for (key, at), copy in flights.items():
            if at == h - 1:
                copy.wait_send()

    out_row = lax.broadcasted_iota(jnp.int32, (main * ring, ring * main), 0)
    in_row = lax.broadcasted_iota(jnp.int32, (main * ring, ring * main), 1)
    same = (out_row // ring == in_row % main) & (out_row % ring == in_row // main)
    order = jnp.where(same, 1.0, 0.0).astype(BF16)
    rt_ref[: main * ring] = jnp.dot(
        order, rg[...].reshape(ring * main, cols), preferred_element_type=F32
    ).astype(BF16)

    move(psi_chains + tail_chains, last_step)
    for off in there[last_step]:
        unpack(off)
    loads[5].wait()
    lanes = q_ref.shape[3]
    lhs = left_ref[...].reshape(terms * rows, cols)
    block = 2 * lanes
    for half in range(cols // block):
        at = slice(half * block, (half + 1) * block)
        q = jnp.dot(lhs, xh[:, :, at].reshape(ring * rows, block), preferred_element_type=F32) + jnp.dot(
            lhs, xl[:, :, at].reshape(ring * rows, block), preferred_element_type=F32
        )
        for part in range(2):
            q_ref[:, half * 2 + part] = q[:, part * lanes : (part + 1) * lanes].reshape(terms, rows, lanes)

    last = rt_ref.shape[0] - main * ring
    out_row = lax.broadcasted_iota(jnp.int32, (last, ring * 16), 0)
    in_row = lax.broadcasted_iota(jnp.int32, (last, ring * 16), 1)
    for n in range(wide):
        same = (out_row % ring == in_row // 16) & ((out_row // ring) * wide + n == in_row % 16) & (in_row % 16 < used_rows)
        order = jnp.where(same, 1.0, 0.0).astype(BF16)
        rt_ref[main * ring :, n * 128 : (n + 1) * 128] = jnp.dot(
            order, rg_last[...].reshape(ring * 16, 128), preferred_element_type=F32
        ).astype(BF16)

    for (key, at), copy in flights.items():
        if at >= max(last_step, right_last) - 1:
            copy.wait_send()


def combine_kernel(unroll, q_ref, pk_ref, b0_ref, b1_ref):
    lanes = q_ref.shape[-1]
    per = lanes // 8
    b0_ref[...] = jnp.zeros_like(b0_ref)
    b1_ref[...] = jnp.zeros_like(b1_ref)
    shape = q_ref.shape[1:]
    group = lax.broadcasted_iota(jnp.int32, shape, 2) // per

    def step(line, n, carry):
        moved = []
        for u in range(unroll):
            word = pk_ref[line, n * unroll + u]
            block = q_ref[word & 255].reshape(shape[0] * shape[1], lanes)
            block = pltpu.roll(block, (word >> 16) & 127, axis=1).reshape(shape)
            moved.append(((word >> 8) & 255, jnp.where(group == (word >> 24), block, 0.0)))
        for u, (place, block) in enumerate(moved):
            b_ref = (b0_ref, b1_ref)[u % 2]
            b_ref[place] = b_ref[place] + block
        return carry

    for line in range(pk_ref.shape[0]):
        lax.fori_loop(0, pk_ref.shape[1] // unroll, functools.partial(step, line), 0)


def scatter_kernel(b0_ref, b1_ref, rt_ref, o_ref, mine, pair, acc, coded, steps, xa, yb, xs, ys, ca, cb, ya, xb, send, recv):
    g = lax.axis_index("sec")
    core = lax.rem(g, 2)
    x = lax.rem(g // 2, 4)
    y = g // 8
    sibling = g + 1 - 2 * core
    half = o_ref.shape[1] // 2
    tiles = b0_ref.shape[2]

    def x_peer(d):
        return (y * 4 + lax.rem(x + d, 4)) * 2 + core

    def y_peer(d):
        return (lax.rem(y + d, 4) * 4 + x) * 2 + core

    barrier = pltpu.get_barrier_semaphore()
    peers = [sibling] + [x_peer(d) for d in (1, 2, 3)] + [y_peer(d) for d in (1, 2, 3)]
    for to in peers:
        pl.semaphore_signal(barrier, inc=1, device_id={"sec": to}, device_id_type=MESH)

    def product(parity, k):
        at = pl.ds(k * half, half)
        b = jnp.concatenate(
            [b0_ref[:, parity, n, at] + b1_ref[:, parity, n, at] for n in range(tiles)], axis=2
        )
        b = b.reshape(b.shape[0] * half, b.shape[2])
        top = b.astype(BF16)
        rest = (b - top.astype(F32)).astype(BF16)
        return jnp.dot(top, rt_ref[...], preferred_element_type=F32) + jnp.dot(
            rest, rt_ref[...], preferred_element_type=F32
        )

    def copy(src, dst, index, to):
        made = pltpu.make_async_remote_copy(
            src_ref=src,
            dst_ref=dst,
            send_sem=send.at[index],
            recv_sem=recv.at[index],
            device_id={"sec": to},
            device_id_type=MESH,
        )
        made.start()
        return made

    steps[...] = jnp.zeros_like(steps)
    first, second, scales, third = [], [], [], []

    def decoded(values, scale):
        return [values[n].astype(jnp.int32).astype(F32) * scale[n : n + 1, :1] for n in range(4)]

    for k in range(2):
        mine[k] = product(1 - core, k).reshape(mine.shape[1:])
        if k == 0:
            pl.semaphore_wait(barrier, len(peers))
        first.append(copy(mine.at[k], pair.at[k], k, sibling))
    for k in range(2):
        own = product(core, k).reshape(acc.shape[1:])
        first[k].wait_recv()
        acc[k] = own + pair[k].reshape(acc.shape[1:])
        for n in range(16):
            part = acc[k, n // 4, n % 4]
            most = jnp.max(jnp.max(jnp.abs(part), axis=0, keepdims=True), axis=1, keepdims=True)
            scale = most * (1.01 / 32767)
            inverse = jnp.where(scale > 0, 1.0 / jnp.where(scale > 0, scale, 1.0), 0.0)
            coded[k, n // 4, n % 4] = jnp.round(part * inverse).astype(jnp.int32).astype(jnp.int16)
            wide = jnp.broadcast_to(scale, (1, 128))
            if k == 0:
                steps[k, n % 4, pl.ds(n // 4, 1), :] = wide
            else:
                steps[k, n // 4, pl.ds(n % 4, 1), :] = wide
        for d in (2, 1, 3):
            index = 2 + k * 3 + d - 1
            if k == 0:
                to = lax.rem(x + d, 4)
                second.append(copy(coded.at[0, :, to], xa.at[d - 1], index, x_peer(d)))
                scales.append(copy(steps.at[0, to], xs.at[d - 1], index + 12, x_peer(d)))
            else:
                to = lax.rem(y + d, 4)
                second.append(copy(coded.at[1, to], yb.at[d - 1], index, y_peer(d)))
                scales.append(copy(steps.at[1, to], ys.at[d - 1], index + 12, y_peer(d)))
    for k in range(2):
        for d in (1, 2, 3):
            second[k * 3 + d - 1].wait_recv()
            scales[k * 3 + d - 1].wait_recv()
        if k == 0:
            parts = [decoded(xa[d], xs[d]) for d in range(3)]
            for n in range(4):
                ca[n] = acc[0, n, x] + parts[0][n] + parts[1][n] + parts[2][n]
        else:
            parts = [decoded(yb[d], ys[d]) for d in range(3)]
            for n in range(4):
                cb[n] = acc[1, y, n] + parts[0][n] + parts[1][n] + parts[2][n]
        for d in (2, 1, 3):
            index = 8 + k * 3 + d - 1
            if k == 0:
                third.append(copy(ca.at[lax.rem(y + d, 4)], ya.at[d - 1], index, y_peer(d)))
            else:
                third.append(copy(cb.at[lax.rem(x + d, 4)], xb.at[d - 1], index, x_peer(d)))
    for k in range(2):
        for d in (1, 2, 3):
            third[k * 3 + d - 1].wait_recv()
        if k == 0:
            o_ref[0, :half] = ca[y] + ya[0] + ya[1] + ya[2]
        else:
            o_ref[0, half:] = cb[x] + xb[0] + xb[1] + xb[2]
    for made in first + second + scales + third:
        made.wait_send()


def body(wavefunction, left_env, right_env, task_in, task_out, task_term):
    groups = lax.axis_size("sec")
    ring = lax.axis_size("env")
    _, rows, cols = wavefunction.shape
    terms = left_env.shape[0]
    per = cols // groups
    padded = -(-terms // 16) * 16
    tiles = -(-terms // 8)
    limit = 40 * 2**20
    sems = pltpu.SemaphoreType.DMA
    ids = (task_in.shape[0] // 128, 128)
    hbm = pl.BlockSpec(memory_space=pltpu.HBM)

    q, rt, packed = pl.pallas_call(
        functools.partial(gather_kernel, groups, ring),
        out_shape=(
            jax.ShapeDtypeStruct((terms, groups // 8, rows, 128), F32),
            jax.ShapeDtypeStruct((tiles * 128, cols), BF16),
            jax.ShapeDtypeStruct(ids, jnp.int32),
        ),
        in_specs=[hbm] * 6,
        out_specs=(vmem(), vmem(), vmem()),
        scratch_shapes=[
            pltpu.VMEM(wavefunction.shape, F32),
            pltpu.VMEM(left_env.shape, BF16),
            pltpu.VMEM(right_env.shape, BF16),
            pltpu.VMEM((3, *ids), jnp.int32),
            pltpu.VMEM((cols, 128), F32),
            pltpu.VMEM((groups, per, 128), BF16),
            pltpu.VMEM((groups, per, 128), BF16),
            pltpu.VMEM((ring, rows, cols), jnp.int16),
            pltpu.VMEM((ring, terms // 16 * 16, cols), BF16),
            pltpu.VMEM((ring, 16, 128), BF16),
            pltpu.VMEM((padded, cols), F32),
            pltpu.VMEM((ring, rows, cols), BF16),
            pltpu.VMEM((ring, rows, cols), BF16),
            sems((groups,)),
            sems((groups,)),
            sems((8 * ring,)),
            sems((8 * ring,)),
            sems((6,)),
        ],
        compiler_params=pltpu.CompilerParams(collective_id=0, has_side_effects=True, vmem_limit_bytes=limit),
        name="gather_psi",
    )(*(
        pltpu.with_memory_space_constraint(a, pltpu.HBM)
        for a in (wavefunction, left_env, right_env, task_in.reshape(ids), task_out.reshape(ids), task_term.reshape(ids))
    ))

    sums = jax.ShapeDtypeStruct((groups * tiles, rows // 8, 8, 128), F32)
    even, odd = pl.pallas_call(
        functools.partial(combine_kernel, 128),
        out_shape=(sums, sums),
        in_specs=[vmem(), pl.BlockSpec(memory_space=pltpu.SMEM)],
        out_specs=(vmem(), vmem()),
        compiler_params=pltpu.CompilerParams(vmem_limit_bytes=limit),
        name="combine_tasks",
    )(q.reshape(terms * (groups // 8), rows // 8, 8, 128), packed)

    half = rows // 2
    split = (groups // 2, 2, tiles, rows, 128)
    return pl.pallas_call(
        scatter_kernel,
        out_shape=jax.ShapeDtypeStruct((1, rows, cols), F32),
        in_specs=[vmem()] * 3,
        out_specs=vmem(),
        scratch_shapes=[
            pltpu.VMEM((2, 16, half, cols), F32),
            pltpu.VMEM((2, 16, half, cols), F32),
            pltpu.VMEM((2, 4, 4, half, cols), F32),
            pltpu.VMEM((2, 4, 4, half, cols), jnp.int16),
            pltpu.VMEM((2, 4, 8, 128), F32),
            pltpu.VMEM((3, 4, half, cols), jnp.int16),
            pltpu.VMEM((3, 4, half, cols), jnp.int16),
            pltpu.VMEM((3, 8, 128), F32),
            pltpu.VMEM((3, 8, 128), F32),
            pltpu.VMEM((4, half, cols), F32),
            pltpu.VMEM((4, half, cols), F32),
            pltpu.VMEM((3, half, cols), F32),
            pltpu.VMEM((3, half, cols), F32),
            sems((20,)),
            sems((20,)),
        ],
        compiler_params=pltpu.CompilerParams(collective_id=1, has_side_effects=True, vmem_limit_bytes=limit),
        name="scatter_sums",
    )(even.reshape(split), odd.reshape(split), rt)


def solution(mesh):
    placed = (P("sec", "env", None), P(None, "env", None), P(None, "env", None), P(), P(), P())
    return jax.shard_map(
        body, mesh=mesh, in_specs=placed, out_specs=P("sec", "env", None), check_vma=False
    )
```

```python
import functools

import jax
import jax.numpy as jnp
from jax import lax
from jax.experimental import pallas as pl
from jax.experimental.pallas import tpu as pltpu
from jax.sharding import PartitionSpec as P

MESH = pl.DeviceIdType.MESH
F32 = jnp.float32
BF16 = jnp.bfloat16


def vmem():
    return pl.BlockSpec(memory_space=pltpu.VMEM)


def gather_kernel(groups, ring, psi_hbm, left_hbm, right_hbm, in_hbm, out_hbm, term_hbm, q_ref, rt_ref, pk_ref,
                  psi_ref, left_ref, right_ref, ids, t_scr, send_buf, got, hl, rg, rg_last, rrow, xh, xl,
                  a_send, a_recv, z_send, z_recv, local):
    g = lax.axis_index("sec")
    e = lax.axis_index("env")
    terms = left_ref.shape[0]
    rows = psi_ref.shape[1]
    cols = psi_ref.shape[2]
    per = cols // groups
    right = lax.rem(e + 1, ring)
    left = lax.rem(e + ring - 1, ring)
    steps = ring // 2
    psi_starts = (1, 5)
    right_starts = (1, 5)
    leaps = sorted({1, *psi_starts, *right_starts})

    loads = [
        pltpu.make_async_copy(src, dst, local.at[n])
        for n, (src, dst) in enumerate(
            (
                (psi_hbm, psi_ref),
                (right_hbm, right_ref),
                (in_hbm, ids.at[0]),
                (out_hbm, ids.at[1]),
                (term_hbm, ids.at[2]),
                (left_hbm, left_ref),
            )
        )
    ]
    for load in loads:
        load.start()

    barrier = pltpu.get_barrier_semaphore()
    for d in range(1, groups):
        pl.semaphore_signal(barrier, inc=1, device_id={"sec": lax.rem(g + d, groups)}, device_id_type=MESH)
    for to in [lax.rem(e + leap, ring) for leap in (*leaps, *(ring - leap for leap in leaps))]:
        pl.semaphore_signal(barrier, inc=1, device_id={"env": to}, device_id_type=MESH)

    loads[0].wait()
    psi = psi_ref[0]
    high = psi.astype(BF16)
    low = (psi - high.astype(F32)).astype(BF16)
    stacked = jnp.concatenate(
        [high.astype(F32), low.astype(F32), jnp.zeros((128 - 2 * rows, cols), F32)], axis=0
    )
    t_scr[...] = stacked.T
    for p in range(groups):
        send_buf[p] = t_scr[pl.ds(p, per, stride=groups), :].astype(BF16)

    pl.semaphore_wait(barrier, groups - 1 + 2 * len(leaps))

    spread = []
    for d in range(1, groups):
        to = lax.rem(g + d, groups)
        copy = pltpu.make_async_remote_copy(
            src_ref=send_buf.at[to],
            dst_ref=got.at[g],
            send_sem=a_send.at[d],
            recv_sem=a_recv.at[d],
            device_id={"sec": to},
            device_id_type=MESH,
        )
        copy.start()
        spread.append(copy)
    got[g] = send_buf[g]

    main = rg.shape[1]
    loads[1].wait()
    rrow[...] = jnp.zeros_like(rrow)
    pick = lax.broadcasted_iota(jnp.int32, (rows, cols), 0) == g
    for w in range(terms):
        row = jnp.sum(jnp.where(pick, right_ref[w].astype(F32), 0.0), axis=0, keepdims=True)
        rrow[pl.ds(w, 1), :] = row
    rg[e] = rrow[:main].astype(BF16)

    flights = {}
    used = []

    def forward(chain, h):
        key, buffer, hops, place, _ = chain
        if (key, h - 1) in flights:
            flights[key, h - 1].wait_recv()
        if h < hops:
            off, to = place(h)
            part = buffer.at[lax.rem(e + off + ring, ring)]
            index = len(used)
            used.append(index)
            copy = pltpu.make_async_remote_copy(
                src_ref=part,
                dst_ref=part,
                send_sem=z_send.at[index],
                recv_sem=z_recv.at[index],
                device_id={"env": to},
                device_id_type=MESH,
            )
            copy.start()
            flights[key, h] = copy

    def chains(key, buffer, starts):
        made = []
        for n in range(len(starts) - 1, -1, -1):
            o = starts[n]
            for sign, end in ((1, steps + 1), (-1, steps)):
                stop = min(starts[n + 1], end) if n + 1 < len(starts) else end
                beside = right if sign > 0 else left
                seed = lax.rem(e + sign * o + ring, ring)
                place = functools.partial(
                    lambda sign, o, seed, beside, h: (-sign * (o + h - 1), beside) if h else (0, seed),
                    sign, o, seed, beside,
                )
                made.append((key + str(sign * o), buffer, stop - o, place, [-sign * k for k in range(o, stop)]))
        return made

    psi_chains = chains("p", hl, psi_starts)
    tail_chains = chains("t", rg_last, psi_starts)
    right_chains = chains("m", rg, right_starts)
    last_step = max(chain[2] for chain in psi_chains)
    right_last = max(chain[2] for chain in right_chains)

    def move(group, h):
        for chain in group:
            forward(chain, h)

    move(right_chains, 0)

    for load in loads[2:5]:
        load.wait()
    s, r, w = ids[0], ids[1], ids[2]
    pk_ref[...] = (
        w * 4 + (s >> 3)
        + ((r * (rt_ref.shape[0] // 128) + (w >> 3)) << 8)
        + ((((w - s) & 7) * (128 // 8)) << 16)
        + ((w & 7) << 24)
    )

    for copy in spread:
        copy.wait_recv()
    back = got[...].astype(F32).reshape(groups * per, 128).T
    block = back[:rows] + back[rows : 2 * rows]
    most = jnp.max(jnp.abs(block), axis=0, keepdims=True)
    scale = (most * (1.01 / 32767)).astype(BF16).astype(F32)
    inverse = jnp.where(scale > 0, 1.0 / jnp.where(scale > 0, scale, 1.0), 0.0)
    hl[e] = jnp.round(block * inverse).astype(jnp.int32).astype(jnp.int16)
    wide = cols // 128
    used_rows = wide * (terms - main)
    tail = jnp.concatenate(
        [rrow[pl.ds(main + n // wide, 1), (n % wide) * 128 : (n % wide + 1) * 128] for n in range(used_rows)]
        + [scale[:, n * 128 : (n + 1) * 128] for n in range(wide)]
        + [jnp.zeros((16 - used_rows - wide, 128), F32)],
        axis=0,
    )
    rg_last[e] = tail.astype(BF16)

    def unpack(off):
        slot = lax.rem(e + off + ring, ring)
        tail = rg_last[slot].astype(F32)
        scale = jnp.concatenate([tail[used_rows + n : used_rows + n + 1] for n in range(wide)], axis=1)
        x = hl[slot].astype(jnp.int32).astype(F32) * scale
        high = x.astype(BF16)
        xh[slot] = high
        xl[slot] = (x - high.astype(F32)).astype(BF16)

    there = [[0]] + [[] for _ in range(last_step)]
    for chain in psi_chains:
        for h, off in enumerate(chain[4]):
            there[h + 1].append(off)
    for h in range(max(last_step, right_last)):
        if h < last_step:
            move(psi_chains + tail_chains, h)
        move(right_chains, h + 1)
        if h < last_step:
            for off in there[h]:
                unpack(off)
        if h == 0:
            for copy in spread:
                copy.wait_send()
        for (key, at), copy in flights.items():
            if at == h - 1:
                copy.wait_send()

    out_row = lax.broadcasted_iota(jnp.int32, (main * ring, ring * main), 0)
    in_row = lax.broadcasted_iota(jnp.int32, (main * ring, ring * main), 1)
    same = (out_row // ring == in_row % main) & (out_row % ring == in_row // main)
    order = jnp.where(same, 1.0, 0.0).astype(BF16)
    rt_ref[: main * ring] = jnp.dot(
        order, rg[...].reshape(ring * main, cols), preferred_element_type=F32
    ).astype(BF16)

    move(psi_chains + tail_chains, last_step)
    for off in there[last_step]:
        unpack(off)
    loads[5].wait()
    lanes = q_ref.shape[3]
    lhs = left_ref[...].reshape(terms * rows, cols)
    block = 2 * lanes
    for half in range(cols // block):
        at = slice(half * block, (half + 1) * block)
        q = jnp.dot(lhs, xh[:, :, at].reshape(ring * rows, block), preferred_element_type=F32) + jnp.dot(
            lhs, xl[:, :, at].reshape(ring * rows, block), preferred_element_type=F32
        )
        for part in range(2):
            q_ref[:, half * 2 + part] = q[:, part * lanes : (part + 1) * lanes].reshape(terms, rows, lanes)

    last = rt_ref.shape[0] - main * ring
    out_row = lax.broadcasted_iota(jnp.int32, (last, ring * 16), 0)
    in_row = lax.broadcasted_iota(jnp.int32, (last, ring * 16), 1)
    for n in range(wide):
        same = (out_row % ring == in_row // 16) & ((out_row // ring) * wide + n == in_row % 16) & (in_row % 16 < used_rows)
        order = jnp.where(same, 1.0, 0.0).astype(BF16)
        rt_ref[main * ring :, n * 128 : (n + 1) * 128] = jnp.dot(
            order, rg_last[...].reshape(ring * 16, 128), preferred_element_type=F32
        ).astype(BF16)

    for (key, at), copy in flights.items():
        if at >= max(last_step, right_last) - 1:
            copy.wait_send()


def combine_kernel(unroll, q_ref, pk_ref, b0_ref, b1_ref):
    lanes = q_ref.shape[-1]
    per = lanes // 8
    b0_ref[...] = jnp.zeros_like(b0_ref)
    b1_ref[...] = jnp.zeros_like(b1_ref)
    shape = q_ref.shape[1:]
    group = lax.broadcasted_iota(jnp.int32, shape, 2) // per

    def step(line, n, carry):
        moved = []
        for u in range(unroll):
            word = pk_ref[line, n * unroll + u]
            block = q_ref[word & 255].reshape(shape[0] * shape[1], lanes)
            block = pltpu.roll(block, (word >> 16) & 127, axis=1).reshape(shape)
            moved.append(((word >> 8) & 255, jnp.where(group == (word >> 24), block, 0.0)))
        for u, (place, block) in enumerate(moved):
            b_ref = (b0_ref, b1_ref)[u % 2]
            b_ref[place] = b_ref[place] + block
        return carry

    for line in range(pk_ref.shape[0]):
        lax.fori_loop(0, pk_ref.shape[1] // unroll, functools.partial(step, line), 0)


def scatter_kernel(b0_ref, b1_ref, rt_ref, o_ref, mine, pair, mine_steps, pair_steps, acc, coded, steps, xa, yb, xs, ys, ca, cb, ya, xb, send, recv):
    g = lax.axis_index("sec")
    core = lax.rem(g, 2)
    x = lax.rem(g // 2, 4)
    y = g // 8
    sibling = g + 1 - 2 * core
    half = o_ref.shape[1] // 2
    tiles = b0_ref.shape[2]

    def x_peer(d):
        return (y * 4 + lax.rem(x + d, 4)) * 2 + core

    def y_peer(d):
        return (lax.rem(y + d, 4) * 4 + x) * 2 + core

    barrier = pltpu.get_barrier_semaphore()
    peers = [sibling] + [x_peer(d) for d in (1, 2, 3)] + [y_peer(d) for d in (1, 2, 3)]
    for to in peers:
        pl.semaphore_signal(barrier, inc=1, device_id={"sec": to}, device_id_type=MESH)

    def product(parity, k):
        at = pl.ds(k * half, half)
        b = jnp.concatenate(
            [b0_ref[:, parity, n, at] + b1_ref[:, parity, n, at] for n in range(tiles)], axis=2
        )
        b = b.reshape(b.shape[0] * half, b.shape[2])
        top = b.astype(BF16)
        rest = (b - top.astype(F32)).astype(BF16)
        return jnp.dot(top, rt_ref[...], preferred_element_type=F32) + jnp.dot(
            rest, rt_ref[...], preferred_element_type=F32
        )

    def copy(src, dst, index, to):
        made = pltpu.make_async_remote_copy(
            src_ref=src,
            dst_ref=dst,
            send_sem=send.at[index],
            recv_sem=recv.at[index],
            device_id={"sec": to},
            device_id_type=MESH,
        )
        made.start()
        return made

    steps[...] = jnp.zeros_like(steps)
    first, second, scales, third = [], [], [], []

    def code(part):
        most = jnp.max(jnp.max(jnp.abs(part), axis=0, keepdims=True), axis=1, keepdims=True)
        scale = most * (1.01 / 32767)
        inverse = jnp.where(scale > 0, 1.0 / jnp.where(scale > 0, scale, 1.0), 0.0)
        return scale, jnp.round(part * inverse).astype(jnp.int32).astype(jnp.int16)

    def decoded(values, scale):
        return [values[n].astype(jnp.int32).astype(F32) * scale[n : n + 1, :1] for n in range(4)]

    for k in range(2):
        theirs = product(1 - core, k).reshape(mine.shape[1:])
        for n in range(16):
            scale, mine[k, n] = code(theirs[n])
            mine_steps[k, pl.ds(n, 1), :] = jnp.broadcast_to(scale, (1, 128))
        if k == 0:
            pl.semaphore_wait(barrier, len(peers))
        first.append(copy(mine.at[k], pair.at[k], k, sibling))
        scales.append(copy(mine_steps.at[k], pair_steps.at[k], 20 + k, sibling))
    for k in range(2):
        own = product(core, k).reshape(mine.shape[1:])
        first[k].wait_recv()
        scales[k].wait_recv()
        for n in range(16):
            arrived = pair[k, n].astype(jnp.int32).astype(F32) * pair_steps[k, n : n + 1, :1]
            acc[k, n // 4, n % 4] = own[n] + arrived
        for n in range(16):
            part = acc[k, n // 4, n % 4]
            scale, coded[k, n // 4, n % 4] = code(part)
            wide = jnp.broadcast_to(scale, (1, 128))
            if k == 0:
                steps[k, n % 4, pl.ds(n // 4, 1), :] = wide
            else:
                steps[k, n // 4, pl.ds(n % 4, 1), :] = wide
        for d in (2, 1, 3):
            index = 2 + k * 3 + d - 1
            if k == 0:
                to = lax.rem(x + d, 4)
                second.append(copy(coded.at[0, :, to], xa.at[d - 1], index, x_peer(d)))
                scales.append(copy(steps.at[0, to], xs.at[d - 1], index + 12, x_peer(d)))
            else:
                to = lax.rem(y + d, 4)
                second.append(copy(coded.at[1, to], yb.at[d - 1], index, y_peer(d)))
                scales.append(copy(steps.at[1, to], ys.at[d - 1], index + 12, y_peer(d)))
    for k in range(2):
        for d in (1, 2, 3):
            second[k * 3 + d - 1].wait_recv()
            scales[2 + k * 3 + d - 1].wait_recv()
        if k == 0:
            parts = [decoded(xa[d], xs[d]) for d in range(3)]
            for n in range(4):
                ca[n] = acc[0, n, x] + parts[0][n] + parts[1][n] + parts[2][n]
        else:
            parts = [decoded(yb[d], ys[d]) for d in range(3)]
            for n in range(4):
                cb[n] = acc[1, y, n] + parts[0][n] + parts[1][n] + parts[2][n]
        for d in (2, 1, 3):
            index = 8 + k * 3 + d - 1
            if k == 0:
                third.append(copy(ca.at[lax.rem(y + d, 4)], ya.at[d - 1], index, y_peer(d)))
            else:
                third.append(copy(cb.at[lax.rem(x + d, 4)], xb.at[d - 1], index, x_peer(d)))
    for k in range(2):
        for d in (1, 2, 3):
            third[k * 3 + d - 1].wait_recv()
        if k == 0:
            o_ref[0, :half] = ca[y] + ya[0] + ya[1] + ya[2]
        else:
            o_ref[0, half:] = cb[x] + xb[0] + xb[1] + xb[2]
    for made in first + second + scales + third:
        made.wait_send()


def body(wavefunction, left_env, right_env, task_in, task_out, task_term):
    groups = lax.axis_size("sec")
    ring = lax.axis_size("env")
    _, rows, cols = wavefunction.shape
    terms = left_env.shape[0]
    per = cols // groups
    padded = -(-terms // 16) * 16
    tiles = -(-terms // 8)
    limit = 40 * 2**20
    sems = pltpu.SemaphoreType.DMA
    ids = (task_in.shape[0] // 128, 128)
    hbm = pl.BlockSpec(memory_space=pltpu.HBM)

    q, rt, packed = pl.pallas_call(
        functools.partial(gather_kernel, groups, ring),
        out_shape=(
            jax.ShapeDtypeStruct((terms, groups // 8, rows, 128), F32),
            jax.ShapeDtypeStruct((tiles * 128, cols), BF16),
            jax.ShapeDtypeStruct(ids, jnp.int32),
        ),
        in_specs=[hbm] * 6,
        out_specs=(vmem(), vmem(), vmem()),
        scratch_shapes=[
            pltpu.VMEM(wavefunction.shape, F32),
            pltpu.VMEM(left_env.shape, BF16),
            pltpu.VMEM(right_env.shape, BF16),
            pltpu.VMEM((3, *ids), jnp.int32),
            pltpu.VMEM((cols, 128), F32),
            pltpu.VMEM((groups, per, 128), BF16),
            pltpu.VMEM((groups, per, 128), BF16),
            pltpu.VMEM((ring, rows, cols), jnp.int16),
            pltpu.VMEM((ring, terms // 16 * 16, cols), BF16),
            pltpu.VMEM((ring, 16, 128), BF16),
            pltpu.VMEM((padded, cols), F32),
            pltpu.VMEM((ring, rows, cols), BF16),
            pltpu.VMEM((ring, rows, cols), BF16),
            sems((groups,)),
            sems((groups,)),
            sems((8 * ring,)),
            sems((8 * ring,)),
            sems((6,)),
        ],
        compiler_params=pltpu.CompilerParams(collective_id=0, has_side_effects=True, vmem_limit_bytes=limit),
        name="gather_psi",
    )(*(
        pltpu.with_memory_space_constraint(a, pltpu.HBM)
        for a in (wavefunction, left_env, right_env, task_in.reshape(ids), task_out.reshape(ids), task_term.reshape(ids))
    ))

    sums = jax.ShapeDtypeStruct((groups * tiles, rows // 8, 8, 128), F32)
    even, odd = pl.pallas_call(
        functools.partial(combine_kernel, 128),
        out_shape=(sums, sums),
        in_specs=[vmem(), pl.BlockSpec(memory_space=pltpu.SMEM)],
        out_specs=(vmem(), vmem()),
        compiler_params=pltpu.CompilerParams(vmem_limit_bytes=limit),
        name="combine_tasks",
    )(q.reshape(terms * (groups // 8), rows // 8, 8, 128), packed)

    half = rows // 2
    split = (groups // 2, 2, tiles, rows, 128)
    return pl.pallas_call(
        scatter_kernel,
        out_shape=jax.ShapeDtypeStruct((1, rows, cols), F32),
        in_specs=[vmem()] * 3,
        out_specs=vmem(),
        scratch_shapes=[
            pltpu.VMEM((2, 16, half, cols), jnp.int16),
            pltpu.VMEM((2, 16, half, cols), jnp.int16),
            pltpu.VMEM((2, 16, 128), F32),
            pltpu.VMEM((2, 16, 128), F32),
            pltpu.VMEM((2, 4, 4, half, cols), F32),
            pltpu.VMEM((2, 4, 4, half, cols), jnp.int16),
            pltpu.VMEM((2, 4, 8, 128), F32),
            pltpu.VMEM((3, 4, half, cols), jnp.int16),
            pltpu.VMEM((3, 4, half, cols), jnp.int16),
            pltpu.VMEM((3, 8, 128), F32),
            pltpu.VMEM((3, 8, 128), F32),
            pltpu.VMEM((4, half, cols), F32),
            pltpu.VMEM((4, half, cols), F32),
            pltpu.VMEM((3, half, cols), F32),
            pltpu.VMEM((3, half, cols), F32),
            sems((22,)),
            sems((22,)),
        ],
        compiler_params=pltpu.CompilerParams(collective_id=1, has_side_effects=True, vmem_limit_bytes=limit),
        name="scatter_sums",
    )(even.reshape(split), odd.reshape(split), rt)


def solution(mesh):
    placed = (P("sec", "env", None), P(None, "env", None), P(None, "env", None), P(), P(), P())
    return jax.shard_map(
        body, mesh=mesh, in_specs=placed, out_specs=P("sec", "env", None), check_vma=False
    )
```

```python
import functools

import jax
import jax.numpy as jnp
from jax import lax
from jax.experimental import pallas as pl
from jax.experimental.pallas import tpu as pltpu
from jax.sharding import PartitionSpec as P

MESH = pl.DeviceIdType.MESH
F32 = jnp.float32
BF16 = jnp.bfloat16


def vmem():
    return pl.BlockSpec(memory_space=pltpu.VMEM)


def gather_kernel(groups, ring, psi_hbm, left_hbm, right_hbm, in_hbm, out_hbm, term_hbm, q_ref, rt_ref, pk_ref,
                  psi_ref, left_ref, right_ref, ids, t_scr, send_buf, got, hl, rg, rg_last, rrow, xh, xl,
                  a_send, a_recv, z_send, z_recv, local):
    g = lax.axis_index("sec")
    e = lax.axis_index("env")
    terms = left_ref.shape[0]
    rows = psi_ref.shape[1]
    cols = psi_ref.shape[2]
    per = cols // groups
    right = lax.rem(e + 1, ring)
    left = lax.rem(e + ring - 1, ring)
    steps = ring // 2
    psi_starts = (1, 5)
    right_starts = (1, 5)
    leaps = sorted({1, *psi_starts, *right_starts})

    loads = [
        pltpu.make_async_copy(src, dst, local.at[n])
        for n, (src, dst) in enumerate(
            (
                (psi_hbm, psi_ref),
                (right_hbm, right_ref),
                (in_hbm, ids.at[0]),
                (out_hbm, ids.at[1]),
                (term_hbm, ids.at[2]),
                (left_hbm, left_ref),
            )
        )
    ]
    for load in loads:
        load.start()

    barrier = pltpu.get_barrier_semaphore()
    for d in range(1, groups):
        pl.semaphore_signal(barrier, inc=1, device_id={"sec": lax.rem(g + d, groups)}, device_id_type=MESH)
    for to in [lax.rem(e + leap, ring) for leap in (*leaps, *(ring - leap for leap in leaps))]:
        pl.semaphore_signal(barrier, inc=1, device_id={"env": to}, device_id_type=MESH)

    loads[0].wait()
    psi = psi_ref[0]
    high = psi.astype(BF16)
    low = (psi - high.astype(F32)).astype(BF16)
    stacked = jnp.concatenate(
        [high.astype(F32), low.astype(F32), jnp.zeros((128 - 2 * rows, cols), F32)], axis=0
    )
    t_scr[...] = stacked.T

    pl.semaphore_wait(barrier, groups - 1 + 2 * len(leaps))

    spread = []
    for d in range(1, groups):
        to = lax.rem(g + d, groups)
        send_buf[to] = t_scr[pl.ds(to, per, stride=groups), :].astype(BF16)
        copy = pltpu.make_async_remote_copy(
            src_ref=send_buf.at[to],
            dst_ref=got.at[g],
            send_sem=a_send.at[d],
            recv_sem=a_recv.at[d],
            device_id={"sec": to},
            device_id_type=MESH,
        )
        copy.start()
        spread.append(copy)
    got[g] = t_scr[pl.ds(g, per, stride=groups), :].astype(BF16)

    main = rg.shape[1]
    loads[1].wait()
    rrow[...] = jnp.zeros_like(rrow)
    pick = lax.broadcasted_iota(jnp.int32, (rows, cols), 0) == g
    for w in range(terms):
        row = jnp.sum(jnp.where(pick, right_ref[w].astype(F32), 0.0), axis=0, keepdims=True)
        rrow[pl.ds(w, 1), :] = row
    rg[e] = rrow[:main].astype(BF16)

    flights = {}
    used = []

    def forward(chain, h):
        key, buffer, hops, place, _ = chain
        if (key, h - 1) in flights:
            flights[key, h - 1].wait_recv()
        if h < hops:
            off, to = place(h)
            part = buffer.at[lax.rem(e + off + ring, ring)]
            index = len(used)
            used.append(index)
            copy = pltpu.make_async_remote_copy(
                src_ref=part,
                dst_ref=part,
                send_sem=z_send.at[index],
                recv_sem=z_recv.at[index],
                device_id={"env": to},
                device_id_type=MESH,
            )
            copy.start()
            flights[key, h] = copy

    def chains(key, buffer, starts):
        made = []
        for n in range(len(starts) - 1, -1, -1):
            o = starts[n]
            for sign, end in ((1, steps + 1), (-1, steps)):
                stop = min(starts[n + 1], end) if n + 1 < len(starts) else end
                beside = right if sign > 0 else left
                seed = lax.rem(e + sign * o + ring, ring)
                place = functools.partial(
                    lambda sign, o, seed, beside, h: (-sign * (o + h - 1), beside) if h else (0, seed),
                    sign, o, seed, beside,
                )
                made.append((key + str(sign * o), buffer, stop - o, place, [-sign * k for k in range(o, stop)]))
        return made

    psi_chains = chains("p", hl, psi_starts)
    tail_chains = chains("t", rg_last, psi_starts)
    right_chains = chains("m", rg, right_starts)
    last_step = max(chain[2] for chain in psi_chains)
    right_last = max(chain[2] for chain in right_chains)

    def move(group, h):
        for chain in group:
            forward(chain, h)

    move(right_chains, 0)

    for load in loads[2:5]:
        load.wait()
    s, r, w = ids[0], ids[1], ids[2]
    pk_ref[...] = (
        w * 4 + (s >> 3)
        + ((r * (rt_ref.shape[0] // 128) + (w >> 3)) << 8)
        + ((((w - s) & 7) * (128 // 8)) << 16)
        + ((w & 7) << 24)
    )

    for copy in spread:
        copy.wait_recv()
    back = got[...].astype(F32).reshape(groups * per, 128).T
    block = back[:rows] + back[rows : 2 * rows]
    most = jnp.max(jnp.abs(block), axis=0, keepdims=True)
    scale = (most * (1.01 / 32767)).astype(BF16).astype(F32)
    inverse = jnp.where(scale > 0, 1.0 / jnp.where(scale > 0, scale, 1.0), 0.0)
    hl[e] = jnp.round(block * inverse).astype(jnp.int32).astype(jnp.int16)
    wide = cols // 128
    used_rows = wide * (terms - main)
    tail = jnp.concatenate(
        [rrow[pl.ds(main + n // wide, 1), (n % wide) * 128 : (n % wide + 1) * 128] for n in range(used_rows)]
        + [scale[:, n * 128 : (n + 1) * 128] for n in range(wide)]
        + [jnp.zeros((16 - used_rows - wide, 128), F32)],
        axis=0,
    )
    rg_last[e] = tail.astype(BF16)

    def unpack(off):
        slot = lax.rem(e + off + ring, ring)
        tail = rg_last[slot].astype(F32)
        scale = jnp.concatenate([tail[used_rows + n : used_rows + n + 1] for n in range(wide)], axis=1)
        x = hl[slot].astype(jnp.int32).astype(F32) * scale
        high = x.astype(BF16)
        xh[slot] = high
        xl[slot] = (x - high.astype(F32)).astype(BF16)

    there = [[0]] + [[] for _ in range(last_step)]
    for chain in psi_chains:
        for h, off in enumerate(chain[4]):
            there[h + 1].append(off)
    for h in range(max(last_step, right_last)):
        if h < last_step:
            move(psi_chains + tail_chains, h)
        move(right_chains, h + 1)
        if h < last_step:
            for off in there[h]:
                unpack(off)
        if h == 0:
            for copy in spread:
                copy.wait_send()
        for (key, at), copy in flights.items():
            if at == h - 1:
                copy.wait_send()

    out_row = lax.broadcasted_iota(jnp.int32, (main * ring, ring * main), 0)
    in_row = lax.broadcasted_iota(jnp.int32, (main * ring, ring * main), 1)
    same = (out_row // ring == in_row % main) & (out_row % ring == in_row // main)
    order = jnp.where(same, 1.0, 0.0).astype(BF16)
    rt_ref[: main * ring] = jnp.dot(
        order, rg[...].reshape(ring * main, cols), preferred_element_type=F32
    ).astype(BF16)

    move(psi_chains + tail_chains, last_step)
    for off in there[last_step]:
        unpack(off)
    loads[5].wait()
    lanes = q_ref.shape[3]
    lhs = left_ref[...].reshape(terms * rows, cols)
    block = 2 * lanes
    for half in range(cols // block):
        at = slice(half * block, (half + 1) * block)
        q = jnp.dot(lhs, xh[:, :, at].reshape(ring * rows, block), preferred_element_type=F32) + jnp.dot(
            lhs, xl[:, :, at].reshape(ring * rows, block), preferred_element_type=F32
        )
        for part in range(2):
            q_ref[:, half * 2 + part] = q[:, part * lanes : (part + 1) * lanes].reshape(terms, rows, lanes)

    last = rt_ref.shape[0] - main * ring
    out_row = lax.broadcasted_iota(jnp.int32, (last, ring * 16), 0)
    in_row = lax.broadcasted_iota(jnp.int32, (last, ring * 16), 1)
    for n in range(wide):
        same = (out_row % ring == in_row // 16) & ((out_row // ring) * wide + n == in_row % 16) & (in_row % 16 < used_rows)
        order = jnp.where(same, 1.0, 0.0).astype(BF16)
        rt_ref[main * ring :, n * 128 : (n + 1) * 128] = jnp.dot(
            order, rg_last[...].reshape(ring * 16, 128), preferred_element_type=F32
        ).astype(BF16)

    for (key, at), copy in flights.items():
        if at >= max(last_step, right_last) - 1:
            copy.wait_send()


def combine_kernel(unroll, q_ref, pk_ref, b0_ref, b1_ref):
    lanes = q_ref.shape[-1]
    per = lanes // 8
    b0_ref[...] = jnp.zeros_like(b0_ref)
    b1_ref[...] = jnp.zeros_like(b1_ref)
    shape = q_ref.shape[1:]
    group = lax.broadcasted_iota(jnp.int32, shape, 2) // per

    def step(line, n, carry):
        moved = []
        for u in range(unroll):
            word = pk_ref[line, n * unroll + u]
            block = q_ref[word & 255].reshape(shape[0] * shape[1], lanes)
            block = pltpu.roll(block, (word >> 16) & 127, axis=1).reshape(shape)
            moved.append(((word >> 8) & 255, jnp.where(group == (word >> 24), block, 0.0)))
        for u, (place, block) in enumerate(moved):
            b_ref = (b0_ref, b1_ref)[u % 2]
            b_ref[place] = b_ref[place] + block
        return carry

    for line in range(pk_ref.shape[0]):
        lax.fori_loop(0, pk_ref.shape[1] // unroll, functools.partial(step, line), 0)


def scatter_kernel(b0_ref, b1_ref, rt_ref, o_ref, mine, pair, mine_steps, pair_steps, acc, coded, steps, xa, yb, xs, ys, ca, cb, ya, xb, send, recv):
    g = lax.axis_index("sec")
    core = lax.rem(g, 2)
    x = lax.rem(g // 2, 4)
    y = g // 8
    sibling = g + 1 - 2 * core
    half = o_ref.shape[1] // 2
    tiles = b0_ref.shape[2]

    def x_peer(d):
        return (y * 4 + lax.rem(x + d, 4)) * 2 + core

    def y_peer(d):
        return (lax.rem(y + d, 4) * 4 + x) * 2 + core

    barrier = pltpu.get_barrier_semaphore()
    peers = [sibling] + [x_peer(d) for d in (1, 2, 3)] + [y_peer(d) for d in (1, 2, 3)]
    for to in peers:
        pl.semaphore_signal(barrier, inc=1, device_id={"sec": to}, device_id_type=MESH)

    def product(parity, k):
        at = pl.ds(k * half, half)
        b = jnp.concatenate(
            [b0_ref[:, parity, n, at] + b1_ref[:, parity, n, at] for n in range(tiles)], axis=2
        )
        b = b.reshape(b.shape[0] * half, b.shape[2])
        top = b.astype(BF16)
        rest = (b - top.astype(F32)).astype(BF16)
        return jnp.dot(top, rt_ref[...], preferred_element_type=F32) + jnp.dot(
            rest, rt_ref[...], preferred_element_type=F32
        )

    def copy(src, dst, index, to):
        made = pltpu.make_async_remote_copy(
            src_ref=src,
            dst_ref=dst,
            send_sem=send.at[index],
            recv_sem=recv.at[index],
            device_id={"sec": to},
            device_id_type=MESH,
        )
        made.start()
        return made

    steps[...] = jnp.zeros_like(steps)
    first, second, scales, third = [], [], [], []

    def code(part):
        most = jnp.max(jnp.max(jnp.abs(part), axis=0, keepdims=True), axis=1, keepdims=True)
        scale = most * (1.01 / 32767)
        inverse = jnp.where(scale > 0, 1.0 / jnp.where(scale > 0, scale, 1.0), 0.0)
        return scale, jnp.round(part * inverse).astype(jnp.int32).astype(jnp.int16)

    def decoded(values, scale):
        return [values[n].astype(jnp.int32).astype(F32) * scale[n : n + 1, :1] for n in range(4)]

    for k in range(2):
        theirs = product(1 - core, k).reshape(mine.shape[1:])
        for n in range(16):
            scale, mine[k, n] = code(theirs[n])
            mine_steps[k, pl.ds(n, 1), :] = jnp.broadcast_to(scale, (1, 128))
        if k == 0:
            pl.semaphore_wait(barrier, len(peers))
        first.append(copy(mine.at[k], pair.at[k], k, sibling))
        scales.append(copy(mine_steps.at[k], pair_steps.at[k], 20 + k, sibling))
    for k in range(2):
        own = product(core, k).reshape(mine.shape[1:])
        first[k].wait_recv()
        scales[k].wait_recv()
        for n in range(16):
            arrived = pair[k, n].astype(jnp.int32).astype(F32) * pair_steps[k, n : n + 1, :1]
            acc[k, n // 4, n % 4] = own[n] + arrived
        for n in range(16):
            part = acc[k, n // 4, n % 4]
            scale, coded[k, n // 4, n % 4] = code(part)
            wide = jnp.broadcast_to(scale, (1, 128))
            if k == 0:
                steps[k, n % 4, pl.ds(n // 4, 1), :] = wide
            else:
                steps[k, n // 4, pl.ds(n % 4, 1), :] = wide
        for d in (2, 1, 3):
            index = 2 + k * 3 + d - 1
            if k == 0:
                to = lax.rem(x + d, 4)
                second.append(copy(coded.at[0, :, to], xa.at[d - 1], index, x_peer(d)))
                scales.append(copy(steps.at[0, to], xs.at[d - 1], index + 12, x_peer(d)))
            else:
                to = lax.rem(y + d, 4)
                second.append(copy(coded.at[1, to], yb.at[d - 1], index, y_peer(d)))
                scales.append(copy(steps.at[1, to], ys.at[d - 1], index + 12, y_peer(d)))
    for k in range(2):
        for d in (1, 2, 3):
            second[k * 3 + d - 1].wait_recv()
            scales[2 + k * 3 + d - 1].wait_recv()
        if k == 0:
            parts = [decoded(xa[d], xs[d]) for d in range(3)]
            for n in range(4):
                ca[n] = acc[0, n, x] + parts[0][n] + parts[1][n] + parts[2][n]
        else:
            parts = [decoded(yb[d], ys[d]) for d in range(3)]
            for n in range(4):
                cb[n] = acc[1, y, n] + parts[0][n] + parts[1][n] + parts[2][n]
        for d in (2, 1, 3):
            index = 8 + k * 3 + d - 1
            if k == 0:
                third.append(copy(ca.at[lax.rem(y + d, 4)], ya.at[d - 1], index, y_peer(d)))
            else:
                third.append(copy(cb.at[lax.rem(x + d, 4)], xb.at[d - 1], index, x_peer(d)))
    for k in range(2):
        for d in (1, 2, 3):
            third[k * 3 + d - 1].wait_recv()
        if k == 0:
            o_ref[0, :half] = ca[y] + ya[0] + ya[1] + ya[2]
        else:
            o_ref[0, half:] = cb[x] + xb[0] + xb[1] + xb[2]
    for made in first + second + scales + third:
        made.wait_send()


def body(wavefunction, left_env, right_env, task_in, task_out, task_term):
    groups = lax.axis_size("sec")
    ring = lax.axis_size("env")
    _, rows, cols = wavefunction.shape
    terms = left_env.shape[0]
    per = cols // groups
    padded = -(-terms // 16) * 16
    tiles = -(-terms // 8)
    limit = 40 * 2**20
    sems = pltpu.SemaphoreType.DMA
    ids = (task_in.shape[0] // 128, 128)
    hbm = pl.BlockSpec(memory_space=pltpu.HBM)

    q, rt, packed = pl.pallas_call(
        functools.partial(gather_kernel, groups, ring),
        out_shape=(
            jax.ShapeDtypeStruct((terms, groups // 8, rows, 128), F32),
            jax.ShapeDtypeStruct((tiles * 128, cols), BF16),
            jax.ShapeDtypeStruct(ids, jnp.int32),
        ),
        in_specs=[hbm] * 6,
        out_specs=(vmem(), vmem(), vmem()),
        scratch_shapes=[
            pltpu.VMEM(wavefunction.shape, F32),
            pltpu.VMEM(left_env.shape, BF16),
            pltpu.VMEM(right_env.shape, BF16),
            pltpu.VMEM((3, *ids), jnp.int32),
            pltpu.VMEM((cols, 128), F32),
            pltpu.VMEM((groups, per, 128), BF16),
            pltpu.VMEM((groups, per, 128), BF16),
            pltpu.VMEM((ring, rows, cols), jnp.int16),
            pltpu.VMEM((ring, terms // 16 * 16, cols), BF16),
            pltpu.VMEM((ring, 16, 128), BF16),
            pltpu.VMEM((padded, cols), F32),
            pltpu.VMEM((ring, rows, cols), BF16),
            pltpu.VMEM((ring, rows, cols), BF16),
            sems((groups,)),
            sems((groups,)),
            sems((8 * ring,)),
            sems((8 * ring,)),
            sems((6,)),
        ],
        compiler_params=pltpu.CompilerParams(collective_id=0, has_side_effects=True, vmem_limit_bytes=limit),
        name="gather_psi",
    )(*(
        pltpu.with_memory_space_constraint(a, pltpu.HBM)
        for a in (wavefunction, left_env, right_env, task_in.reshape(ids), task_out.reshape(ids), task_term.reshape(ids))
    ))

    sums = jax.ShapeDtypeStruct((groups * tiles, rows // 8, 8, 128), F32)
    even, odd = pl.pallas_call(
        functools.partial(combine_kernel, 128),
        out_shape=(sums, sums),
        in_specs=[vmem(), pl.BlockSpec(memory_space=pltpu.SMEM)],
        out_specs=(vmem(), vmem()),
        compiler_params=pltpu.CompilerParams(vmem_limit_bytes=limit),
        name="combine_tasks",
    )(q.reshape(terms * (groups // 8), rows // 8, 8, 128), packed)

    half = rows // 2
    split = (groups // 2, 2, tiles, rows, 128)
    return pl.pallas_call(
        scatter_kernel,
        out_shape=jax.ShapeDtypeStruct((1, rows, cols), F32),
        in_specs=[vmem()] * 3,
        out_specs=vmem(),
        scratch_shapes=[
            pltpu.VMEM((2, 16, half, cols), jnp.int16),
            pltpu.VMEM((2, 16, half, cols), jnp.int16),
            pltpu.VMEM((2, 16, 128), F32),
            pltpu.VMEM((2, 16, 128), F32),
            pltpu.VMEM((2, 4, 4, half, cols), F32),
            pltpu.VMEM((2, 4, 4, half, cols), jnp.int16),
            pltpu.VMEM((2, 4, 8, 128), F32),
            pltpu.VMEM((3, 4, half, cols), jnp.int16),
            pltpu.VMEM((3, 4, half, cols), jnp.int16),
            pltpu.VMEM((3, 8, 128), F32),
            pltpu.VMEM((3, 8, 128), F32),
            pltpu.VMEM((4, half, cols), F32),
            pltpu.VMEM((4, half, cols), F32),
            pltpu.VMEM((3, half, cols), F32),
            pltpu.VMEM((3, half, cols), F32),
            sems((22,)),
            sems((22,)),
        ],
        compiler_params=pltpu.CompilerParams(collective_id=1, has_side_effects=True, vmem_limit_bytes=limit),
        name="scatter_sums",
    )(even.reshape(split), odd.reshape(split), rt)


def solution(mesh):
    placed = (P("sec", "env", None), P(None, "env", None), P(None, "env", None), P(), P(), P())
    return jax.shard_map(
        body, mesh=mesh, in_specs=placed, out_specs=P("sec", "env", None), check_vma=False
    )
```
